32 devices in a mesh: group: 2 (over y), tx: 4 (over z), ty: 2 (over x), ch: 2 (over core).
Axes of the slice: x: 2, y: 2, z: 4, core: 2. Of those that a mesh axis runs over, the one named last changes fastest.
Arguments:
- fine_features: bfloat16 [32, 65536], P('ch', ('group', 'tx', 'ty')), parts along dimension 1, may hold values from -6 to 6
- neighbours: int32 [27, 65536], P(None, ('group', 'tx', 'ty')), parts along dimension 1, may hold values from 0 to 6656, as said below
- face_send: int32 [4, 8192], P(None, ('group', 'tx', 'ty')), parts along dimension 1, may hold values from 0 to 4095
- corner_send: int32 [4, 2048], P(None, ('group', 'tx', 'ty')), parts along dimension 1, may hold values from 0 to 4095
- owner_side: int32 [65536], P(('group', 'tx', 'ty')), parts along dimension 0, may hold values from 0 to 8, as said below
- owner_slot: int32 [65536], P(('group', 'tx', 'ty')), parts along dimension 0, may hold values from 0 to 255
- conv_weight: bfloat16 [27, 32, 32], replicated, may hold values from -0.21875 to 0.21875
- coarse_weight: bfloat16 [32, 128], replicated, may hold values from -0.25 to 0.25
- coarse_grad: bfloat16 [128, 4096], P(None, ('group', 'tx', 'ty')), parts along dimension 1, may hold values from -6 to 6
Outputs:
- coarse_out: bfloat16 [128, 4096], P('ch', ('group', 'tx', 'ty')), parts along dimension 1
- input_grad: bfloat16 [32, 65536], P('ch', ('group', 'tx', 'ty')), parts along dimension 1
- conv_weight_grad: float32 [54, 32, 32], P('group', None, 'ch'), parts along dimension 0
- coarse_weight_grad: float32 [64, 128], P('group', 'ch'), parts along dimension 0
The draws below stay inside these ranges and needn't reach their ends.
There are 2 independent parts, one for each index of `group`. The reference program is written for one: setup_inputs(seed, part) draws one part's arguments, and reference() takes and returns one part's arrays. A program takes and returns all parts, laid end to end along the dimension named above; an argument that names none is the same for every part. Nothing has to cross between parts.
Inputs may be any that keep to these rules, and one draw needn't show every extreme that they name: `neighbours`: entries below 4096 are the tile's own rows, then come four blocks of 512 and four of 128 rows in the order of the steps; the largest value means no neighbour. Entry 13 of every voxel is its own row. `owner_side`: the named tile always exists. Among the rows of one tile every value other than 0 is named at most 256 times, and in every tile some value exactly 256 times.
All inputs are finite; a program needn't handle non-finite values.
Results may differ from the reference program's by a relative error of at most 0.0059.
Values may be sent and summed in bfloat16 or wider, within the bound.
No kernel may reach another device: no remote copies, remote signals or barrier semaphores. Data moves between devices by JAX's collectives and lax.ppermute only.
A program may use at most 64 MiB of HBM per device.

```python
import jax
import jax.numpy as jnp
from jax import lax

C = 32
CC = 128
OFFS = 27
VF = 4096
HF = 512
HC = 128
CV = 256
TILES = 8
MOST = 256
NF = 32768
NC = 2048
EXT = 6784
N_TX = 4
N_TY = 2


TOWARD_X = (-1, 1, 0, 0, -1, -1, 1, 1)


TOWARD_Y = (0, 0, -1, 1, -1, 1, -1, 1)


def draw_neighbours(key, part):
    key = jax.random.fold_in(key, 11)
    first_key, second_key = jax.random.split(key)
    beyond = VF + 4 * HF + 4 * HC
    picked = jax.random.randint(first_key, (OFFS, NF), 0, beyond, dtype=jnp.int32)
    missing = jax.random.randint(second_key, (OFFS, NF), 0, 5, dtype=jnp.int32)
    picked = jnp.where(missing == 0, beyond, picked)
    itself = jnp.arange(NF, dtype=jnp.int32) % VF
    return picked.at[OFFS // 2].set(itself).astype(jnp.int32)


def draw_owner_side(key, part):
    key = jax.random.fold_in(key, 23)
    count_key, order_key = jax.random.split(key)
    tile_count = N_TX * N_TY
    tiles = jnp.arange(tile_count, dtype=jnp.int32)
    pos_x = (tiles // N_TY)[:, None] + jnp.array(TOWARD_X, dtype=jnp.int32)[None, :]
    pos_y = (tiles % N_TY)[:, None] + jnp.array(TOWARD_Y, dtype=jnp.int32)[None, :]
    valid = (pos_x >= 0) & (pos_x < N_TX) & (pos_y >= 0) & (pos_y < N_TY)
    counts = jax.random.randint(count_key, (tile_count, 8), 1, MOST + 1, dtype=jnp.int32)
    first = jnp.argmax(valid.astype(jnp.int32), axis=1)
    chosen = jnp.arange(8, dtype=jnp.int32)[None, :] == first[:, None]
    counts = jnp.where(chosen, MOST, counts)
    counts = jnp.where(valid, counts, 0).astype(jnp.int32)
    bounds = jnp.cumsum(counts, axis=1)
    rows = jnp.arange(VF, dtype=jnp.int32)
    passed = jnp.sum((rows[None, :, None] >= bounds[:, None, :]).astype(jnp.int32), axis=2)
    side = jnp.where(passed == 8, 0, passed + 1).astype(jnp.int32)
    keys = jax.random.split(order_key, tile_count)
    orders = jax.vmap(lambda k: jax.random.permutation(k, VF))(keys).astype(jnp.int32)
    side = jnp.take_along_axis(side, orders, axis=1)
    return side.reshape(-1).astype(jnp.int32)


def touch_ends(entries, rng, low, top_value):
    extent = entries.shape
    index_at = [jax.random.randint(jax.random.fold_in(rng, axis), (), 0, extent[axis]) for axis in range(len(extent))]
    entries = entries.at[tuple(index_at)].set(low)
    longest = extent.index(max(extent))
    index_at[longest] = (index_at[longest] + 1) % extent[longest]
    return entries.at[tuple(index_at)].set(top_value)


def levels(rng, shape, shards, least, largest):
    loudness, own = 1.0, jax.random.fold_in(rng, 6)
    for position, blocks in shards:
        draws = jnp.exp(jax.random.uniform(jax.random.fold_in(own, position), (blocks,), jnp.float32, least / len(shards), largest / len(shards)))
        loudness = loudness * jnp.repeat(draws, shape[position] // blocks).reshape([-1 if axis == position else 1 for axis in range(len(shape))])
    return loudness


def noise(stream_key, extent, width, most, cuts=(), kind=jnp.bfloat16):
    values = jax.random.normal(stream_key, extent, jnp.float32) * width
    if len(cuts) > 0:
        values = levels(stream_key, extent, cuts, -0.22, 0.18) * values
    return jnp.clip(values, min=-most, max=most).astype(kind)


def setup_inputs(seed: int = 0, part: int = 0) -> dict:
    key_list = jax.random.split(jax.random.key(seed), 10)
    part_keys = jax.random.split(jax.random.fold_in(key_list[9], part), 10)
    return {
        "fine_features": noise(part_keys[0], (C, NF), 1.0, 6.0, ((0, 2), (1, 8))),
        "neighbours": draw_neighbours(jax.random.fold_in(jax.random.fold_in(key_list[9], part), 71), part),
        "face_send": touch_ends(jax.random.randint(part_keys[2], (4, HF * TILES), 0, VF), jax.random.fold_in(part_keys[2], 1), 0, VF - 1).astype(jnp.int32),
        "corner_send": touch_ends(jax.random.randint(part_keys[3], (4, HC * TILES), 0, VF), jax.random.fold_in(part_keys[3], 1), 0, VF - 1).astype(jnp.int32),
        "owner_side": draw_owner_side(jax.random.fold_in(jax.random.fold_in(key_list[9], part), 71), part),
        "owner_slot": touch_ends(jax.random.randint(part_keys[5], (NF,), 0, CV), jax.random.fold_in(part_keys[5], 1), 0, CV - 1).astype(jnp.int32),
        "conv_weight": noise(key_list[6], (OFFS, C, C), (OFFS * C) ** -0.5, 0.21875),
        "coarse_weight": noise(key_list[7], (C, CC), (16 * C) ** -0.5, 0.25),
        "coarse_grad": noise(part_keys[8], (CC, NC), 1.0, 6.0, ((1, 8),)),
    }


FACE_STEPS = ((-1, 0), (1, 0), (0, -1), (0, 1))
FACE_OPPOSITE = (1, 0, 3, 2)
CORNER_STEPS = ((-1, -1), (-1, 1), (1, -1), (1, 1))
CORNER_OPPOSITE = (3, 2, 1, 0)
SIDE_X = (0, -1, 1, 0, 0, -1, -1, 1, 1)
SIDE_Y = (0, 0, 0, -1, 1, -1, 1, -1, 1)


def arrivals(packed, offsets, opposite):
    padded = jnp.pad(packed, ((0, 0), (1, 1), (1, 1), (0, 0), (0, 0)))
    pieces = []
    for direction in range(4):
        step_x, step_y = offsets[direction]
        pieces.append(padded[:, 1 + step_x:1 + step_x + N_TX, 1 + step_y:1 + step_y + N_TY, opposite[direction]])
    return jnp.concatenate(pieces, axis=-1)


def packets(tile_grid, send_lists, span_rows):
    ordering = send_lists.reshape(4, N_TX, N_TY, span_rows).transpose(1, 2, 0, 3).reshape(1, N_TX, N_TY, 4 * span_rows)
    ordering = jnp.broadcast_to(ordering, (tile_grid.shape[0], N_TX, N_TY, 4 * span_rows))
    gathered = jnp.take_along_axis(tile_grid, ordering, axis=-1)
    return gathered.reshape(tile_grid.shape[0], N_TX, N_TY, 4, span_rows)


def tile_index(send_lists, span_rows, row_count):
    bases = jnp.arange(TILES, dtype=jnp.int32)[:, None] * row_count
    ordered = send_lists.reshape(4, TILES, span_rows).transpose(1, 0, 2).reshape(TILES, 4 * span_rows)
    return (bases + ordered).reshape(-1).astype(jnp.int32)


def silu_slope(values):
    sigma = jax.nn.sigmoid(values)
    return sigma * (1.0 + values * (1.0 - sigma))


def reference(fine_features, neighbours, face_send, corner_send, owner_side, owner_slot, conv_weight, coarse_weight, coarse_grad):
    tile_grid = fine_features.reshape(C, N_TX, N_TY, VF)
    face_in = arrivals(packets(tile_grid, face_send, HF), FACE_STEPS, FACE_OPPOSITE)
    corner_in = arrivals(packets(tile_grid, corner_send, HC), CORNER_STEPS, CORNER_OPPOSITE)
    padding = jnp.zeros((C, N_TX, N_TY, EXT - VF - 4 * HF - 4 * HC), fine_features.dtype)
    extended = jnp.concatenate([tile_grid, face_in, corner_in, padding], axis=-1)
    neighbour_grid = neighbours.reshape(OFFS, N_TX, N_TY, VF)

    def neighbour_values(offset):
        picker = jnp.broadcast_to(neighbour_grid[offset][None], (C, N_TX, N_TY, VF))
        return jnp.take_along_axis(extended, picker, axis=-1).astype(jnp.float32)

    def forward_step(running, offset):
        weight = conv_weight[offset].astype(jnp.float32)
        return running + jnp.einsum('io,iabv->oabv', weight, neighbour_values(offset)), None

    hidden, _ = lax.scan(forward_step, jnp.zeros((C, N_TX, N_TY, VF), jnp.float32), jnp.arange(OFFS))
    hidden = hidden.reshape(C, NF)
    active = jax.nn.silu(hidden).astype(jnp.bfloat16)
    tile = (jnp.arange(NF, dtype=jnp.int32) // VF).astype(jnp.int32)
    move_x = jnp.array(SIDE_X, dtype=jnp.int32)[owner_side]
    move_y = jnp.array(SIDE_Y, dtype=jnp.int32)[owner_side]
    owner = ((tile // N_TY + move_x) * N_TY + tile % N_TY + move_y).astype(jnp.int32)
    parent = (owner * CV + owner_slot).astype(jnp.int32)
    pooled = jax.ops.segment_sum(active.T.astype(jnp.float32), parent, num_segments=NC).T.astype(jnp.bfloat16)
    coarse_out = jnp.dot(coarse_weight.T, pooled, preferred_element_type=jnp.float32).astype(jnp.bfloat16)
    pooled_grad = jnp.dot(coarse_weight, coarse_grad, preferred_element_type=jnp.float32).astype(jnp.bfloat16)
    active_grad = jnp.take(pooled_grad, parent, axis=1)
    hidden_grad = (active_grad.astype(jnp.float32) * silu_slope(hidden)).astype(jnp.bfloat16)
    grad_grid = hidden_grad.astype(jnp.float32).reshape(C, N_TX, N_TY, VF)

    def weight_step(running, offset):
        return running, jnp.einsum('iabv,oabv->io', neighbour_values(offset), grad_grid)

    _, conv_weight_grad = lax.scan(weight_step, jnp.float32(0.0), jnp.arange(OFFS))
    coarse_weight_grad = jnp.dot(pooled, coarse_grad.T, preferred_element_type=jnp.float32)
    flat_index = (jnp.arange(TILES, dtype=jnp.int32)[None, :, None] * EXT + neighbours.reshape(OFFS, TILES, VF)).reshape(OFFS, NF)
    grad_float = hidden_grad.astype(jnp.float32)

    def input_step(running, offset):
        contrib = jnp.einsum('io,ov->iv', conv_weight[offset].astype(jnp.float32), grad_float)
        return running.at[:, flat_index[offset]].add(contrib), None

    ext_grad, _ = lax.scan(input_step, jnp.zeros((C, TILES * EXT), jnp.float32), jnp.arange(OFFS))
    ext_grad = ext_grad.reshape(C, N_TX, N_TY, EXT)
    face_back = ext_grad[..., VF:VF + 4 * HF].astype(jnp.bfloat16).reshape(C, N_TX, N_TY, 4, HF)
    corner_back = ext_grad[..., VF + 4 * HF:VF + 4 * HF + 4 * HC].astype(jnp.bfloat16).reshape(C, N_TX, N_TY, 4, HC)
    face_ret = arrivals(face_back, FACE_STEPS, FACE_OPPOSITE).reshape(C, -1).astype(jnp.float32)
    corner_ret = arrivals(corner_back, CORNER_STEPS, CORNER_OPPOSITE).reshape(C, -1).astype(jnp.float32)
    own_part = ext_grad[..., :VF].reshape(C, NF)
    own_part = own_part.at[:, tile_index(face_send, HF, VF)].add(face_ret)
    own_part = own_part.at[:, tile_index(corner_send, HC, VF)].add(corner_ret)
    input_grad = own_part.astype(jnp.bfloat16)
    return coarse_out, input_grad, conv_weight_grad, coarse_weight_grad
```

```python
import functools

import jax
import jax.numpy as jnp
from jax import lax
from jax.experimental import pallas as pl
from jax.experimental.pallas import tpu as pltpu
from jax.sharding import PartitionSpec as P

BF = jnp.bfloat16
F32 = jnp.float32
FACE_STEPS = ((-1, 0), (1, 0), (0, -1), (0, 1))
CORNER_STEPS = ((-1, -1), (-1, 1), (1, -1), (1, 1))
LOW = 256
VMEM_LIMIT = 56 << 20


def call(kernel, name, outs, scratch, flops, *args, smem=1):
    specs = [pl.BlockSpec(memory_space=pltpu.SMEM)] * smem
    specs += [pl.BlockSpec(memory_space=pltpu.VMEM)] * (len(args) - smem)
    return pl.pallas_call(
        kernel,
        name=name,
        out_shape=[jax.ShapeDtypeStruct(s, d) for s, d in outs],
        in_specs=specs,
        out_specs=[pl.BlockSpec(memory_space=pltpu.VMEM)] * len(outs),
        scratch_shapes=[pltpu.VMEM(s, d) for s, d in scratch],
        compiler_params=pltpu.CompilerParams(vmem_limit_bytes=VMEM_LIMIT),
        cost_estimate=pl.CostEstimate(flops=flops, bytes_accessed=1 << 20, transcendentals=0),
    )(*args)


class Plan:
    def __init__(self, shapes, nx, ny, nch):
        features, neighbours, face_send, corner_send, coarse_weight, coarse_grad = shapes
        self.nx, self.ny, self.nch = nx, ny, nch
        self.share, self.voxels = features
        self.channels = self.share * nch
        self.offsets = neighbours[0]
        self.half = self.voxels // nch
        self.face, self.corner = face_send[1], corner_send[1]
        self.coarse_channels, self.coarse = coarse_grad
        self.coarse_share = self.coarse_channels // nch
        self.own_blocks = self.voxels // LOW
        self.paired = ny == 2
        self.widths = [self.face] * (3 if self.paired else 4)
        self.widths += [self.corner] * (2 if self.paired else 4)
        self.slots = len(self.widths)
        self.halo = sum(self.widths)
        self.halo_blocks = self.halo // LOW
        self.starts = [sum(self.widths[:s]) for s in range(self.slots)]
        self.nothing = self.voxels + self.halo

    def pairs(self, slot):
        steps = FACE_STEPS + CORNER_STEPS
        if self.paired:
            directions = ((0,), (1,), (2, 3), (4, 5), (6, 7))[slot]
        else:
            directions = (slot,)
        found = []
        for x in range(self.nx):
            for y in range(self.ny):
                for d in directions:
                    sx, sy = x + steps[d][0], y + steps[d][1]
                    if 0 <= sx < self.nx and 0 <= sy < self.ny:
                        found.append((sx * self.ny + sy, x * self.ny + y))
        return found

    def send_rows(self, slot, y, face, corner):
        if not self.paired:
            if slot < 4:
                index = (1, 0, 3, 2)[slot]
                return face[index : index + 1, :]
            index = (3, 2, 1, 0)[slot - 4]
            return corner[index : index + 1, :]
        if slot == 0:
            return face[1:2, :]
        if slot == 1:
            return face[0:1, :]
        if slot == 2:
            return jnp.where(y == 0, face[3:4, :], face[2:3, :])
        if slot == 3:
            return jnp.where(y == 0, corner[3:4, :], corner[2:3, :])
        return jnp.where(y == 0, corner[1:2, :], corner[0:1, :])

    def rows(self, index, y):
        if not self.paired:
            return jnp.minimum(index, self.nothing)
        v, f, c = self.voxels, self.face, self.corner
        along_y = v + 2 * f
        corners = v + 4 * f
        end = corners + 4 * c
        mine = jnp.where(y == 0, along_y + f, along_y)
        of_y = jnp.where((index >= mine) & (index < mine + f), index - mine + along_y, self.nothing)
        result = jnp.where(index < along_y, index, of_y)
        first = jnp.where(y == 0, c, 0)
        at = index - corners - first
        one = jnp.where((at >= 0) & (at < c), at + v + 3 * f, self.nothing)
        two = jnp.where((at >= 2 * c) & (at < 3 * c), at - c + v + 3 * f, one)
        return jnp.where((index >= corners) & (index < end), two, result)

    def owner_slots(self, side):
        if not self.paired:
            return side
        return jnp.where(side < 3, side, jnp.where(side < 5, 3, jnp.where(side < 7, 4, 5)))


def forward(plan, slot, value):
    return lax.ppermute(value, ("tx", "ty"), plan.pairs(slot))


def backward(plan, slot, value):
    return lax.ppermute(value, ("tx", "ty"), [(b, a) for a, b in plan.pairs(slot)])


def lows(low, height, width):
    iota = lax.broadcasted_iota(jnp.int32, (height, width), 0).astype(BF)
    return jnp.where(iota == low, BF(1), BF(0))


def prepare_kernel(plan, place, neighbours, side, slot, high_out, low_out, side_out, slot_out):
    core, y = place[0], place[1]
    mine = pl.ds(pl.multiple_of(core * plan.half, plan.half), plan.half)
    rows = plan.rows(neighbours[:, mine], y)
    pad = high_out.shape[0] - plan.offsets
    fill = jnp.zeros((pad, plan.half), jnp.int32)
    rows = jnp.concatenate([rows, fill], axis=0) if pad else rows
    high_out[...] = lax.shift_right_logical(rows, 8).astype(F32)
    low_out[...] = (rows & (LOW - 1)).astype(F32)
    side_out[...] = plan.owner_slots(side[:, mine]).astype(F32)
    slot_out[...] = slot[:, mine].astype(F32)


def pack_kernel(plan, place, own, other, face, corner, coarse_grad, table, *messages):
    core, y = place[0], place[1]
    s, n = plan.share, plan.channels
    at_own = pl.multiple_of(core * s, s)
    at_other = pl.multiple_of((1 - core) * s, s)
    for b in range(plan.own_blocks):
        table[pl.ds(b * n + at_own, s), :] = own[:, b * LOW : (b + 1) * LOW]
        table[pl.ds(b * n + at_other, s), :] = other[:, b * LOW : (b + 1) * LOW]
    groups = plan.coarse_channels // n
    for k in range(plan.slots):
        width = plan.widths[k]
        rows = plan.send_rows(k, y, face, corner)
        high = lax.shift_right_logical(rows, 8)
        hot = lows((rows & (LOW - 1)).astype(F32).astype(BF), LOW, width)
        part = jnp.dot(table[...], hot, preferred_element_type=F32)
        picked = jnp.zeros((n, width), F32)
        for b in range(plan.own_blocks):
            picked = jnp.where(high == b, part[b * n : (b + 1) * n], picked)
        messages[k][:, :width] = picked.astype(BF)
        for g in range(groups):
            at = width + g * plan.coarse
            messages[k][:, at : at + plan.coarse] = coarse_grad[g * n : (g + 1) * n, :]


def gather_loop(plan, table, high_ref, low_ref, out, base, blocks, before):
    n = plan.channels
    group = 9 if plan.offsets % 9 == 0 else 1
    steps = plan.offsets // group

    def body(step, carry):
        fs = pl.ds(pl.multiple_of((step // steps) * LOW, LOW), LOW)
        for u in range(group):
            k = (step % steps) * group + u
            at = pl.ds(pl.multiple_of(k * n, n), n)
            low = low_ref[pl.ds(k, 1), fs].astype(BF)
            high = high_ref[pl.ds(k, 1), fs]
            part = jnp.dot(table[...], lows(low, LOW, LOW), preferred_element_type=F32)
            if before is None:
                picked = jnp.zeros((n, LOW), F32)
            else:
                picked = before[at, fs].astype(F32)
            for b in range(blocks):
                picked = jnp.where(high == base + b, part[b * n : (b + 1) * n], picked)
            out[at, fs] = picked.astype(BF)
        return carry

    lax.fori_loop(0, plan.half // LOW * steps, body, 0)


def own_gather_kernel(plan, table, high, low, out):
    gather_loop(plan, table, high, low, out, 0, plan.own_blocks, None)


def middle_kernel(plan, place, *refs):
    n, s, m = plan.channels, plan.share, plan.coarse
    messages, refs = refs[: plan.slots], refs[plan.slots :]
    before, high, low, side, slot, weight, coarse_weight, coarse_grad, refs = (*refs[:8], refs[8:])
    grad_out, mine_out, theirs_out, refs = (*refs[:3], refs[3:])
    parts_out, refs = refs[: plan.slots + 1], refs[plan.slots + 1 :]
    table, rows, coarse_all, pooled_all, sums, parts = refs
    core = place[0]
    for k in range(plan.slots):
        for part in range(0, plan.widths[k], min(LOW, plan.widths[k])):
            width = min(LOW, plan.widths[k])
            at = plan.starts[k] + part
            b, column = at // LOW, at % LOW
            table[b * n : (b + 1) * n, column : column + width] = messages[k][:, part : part + width]
    gather_loop(plan, table, high, low, rows, plan.own_blocks, plan.halo_blocks, before)

    groups = plan.coarse_channels // n
    coarse_all[:, :m] = coarse_grad[...]
    for k in range(plan.slots):
        for g in range(groups):
            at = plan.widths[k] + g * m
            coarse_all[g * n : (g + 1) * n, (k + 1) * m : (k + 2) * m] = messages[k][:, at : at + m]
    grads = jnp.dot(coarse_weight[...], coarse_all[...], preferred_element_type=F32).astype(BF)
    owners = plan.slots + 1
    for k in range(owners):
        pooled_all[k * n : (k + 1) * n, :] = grads[:, k * m : (k + 1) * m]
    chunk = min(plan.half, 512)
    wide = plan.offsets * n
    sums[...] = jnp.zeros_like(sums)
    parts[...] = jnp.zeros_like(parts)
    for c in range(plan.half // chunk):
        fs = slice(c * chunk, (c + 1) * chunk)
        picked = rows[:, fs]
        hidden = lax.dot_general(
            weight[...], picked, (((0,), (0,)), ((), ())), preferred_element_type=F32
        )
        sigma = 1.0 / (1.0 + jnp.exp(-hidden))
        active = (hidden * sigma).astype(BF)
        owner = side[:, fs]
        owner_low = owner.astype(BF)
        hot = lows(slot[:, fs].astype(BF), m, chunk)
        spread = jnp.concatenate(
            [jnp.where(owner_low == BF(k), active, BF(0)) for k in range(owners)], axis=0
        )
        parts[...] += lax.dot_general(
            spread, hot, (((1,), (1,)), ((), ())), preferred_element_type=F32
        )
        found = jnp.dot(pooled_all[...], hot, preferred_element_type=F32)
        above = jnp.zeros((n, chunk), F32)
        for k in range(owners):
            above = jnp.where(owner == float(k), found[k * n : (k + 1) * n], above)
        grad = (above * (sigma * (1.0 + hidden * (1.0 - sigma)))).astype(BF)
        grad_out[:, fs] = grad
        sums[:, :wide] += lax.dot_general(
            grad, picked, (((1,), (1,)), ((), ())), preferred_element_type=F32
        )
    total = jnp.zeros((plan.coarse_channels, n), F32)
    for k in range(owners):
        value = parts[k * n : (k + 1) * n, :]
        parts_out[k][...] = value
        first = value.astype(BF)
        second = (value - first.astype(F32)).astype(BF)
        grads_k = coarse_all[:, k * m : (k + 1) * m]
        for piece in (first, second):
            total = total + lax.dot_general(
                grads_k, piece, (((1,), (1,)), ((), ())), preferred_element_type=F32
            )
    pieces = plan.coarse_share // s
    start = sums.shape[1] - pieces * n
    for h in range(plan.nch):
        for q in range(pieces):
            row = h * plan.coarse_share + q * s
            sums[h * s : (h + 1) * s, start + q * n : start + (q + 1) * n] = total[row : row + s]
    mine_out[...] = sums[pl.ds(pl.multiple_of(core * s, s), s), :]
    theirs_out[...] = sums[pl.ds(pl.multiple_of((1 - core) * s, s), s), :]


def scatter_loop(plan, values, high_ref, low_ref, total, base, blocks):
    group = 9 if plan.offsets % 9 == 0 else 1
    steps = plan.offsets // group
    width = min(plan.half, 512)
    n = plan.channels
    total[...] = jnp.zeros_like(total)

    def body(step, carry):
        fs = pl.ds(pl.multiple_of((step // steps) * width, width), width)
        masked, hots = [], []
        for u in range(group):
            k = (step % steps) * group + u
            high = high_ref[pl.ds(k, 1), fs].astype(BF)
            hots.append(lows(low_ref[pl.ds(k, 1), fs].astype(BF), LOW, width))
            value = values[pl.ds(pl.multiple_of(k * n, n), n), fs]
            masked.append(
                jnp.concatenate(
                    [jnp.where(high == BF(base + b), value, BF(0)) for b in range(blocks)], axis=0
                )
            )
        total[...] += lax.dot_general(
            jnp.concatenate(masked, axis=1),
            jnp.concatenate(hots, axis=1),
            (((1,), (1,)), ((), ())),
            preferred_element_type=F32,
        )
        return carry

    lax.fori_loop(0, plan.half // width * steps, body, 0)


def spread_values(plan, weight, grad, values):
    chunk = min(plan.half, 512)
    for c in range(plan.half // chunk):
        fs = slice(c * chunk, (c + 1) * chunk)
        values[:, fs] = jnp.dot(weight[...], grad[:, fs], preferred_element_type=F32).astype(BF)


def halo_scatter_kernel(plan, weight, grad, high, low, *refs):
    outs, (values, total) = refs[: plan.slots], refs[plan.slots :]
    n = plan.channels
    spread_values(plan, weight, grad, values)
    scatter_loop(plan, values, high, low, total, plan.own_blocks, plan.halo_blocks)
    for k in range(plan.slots):
        width = min(LOW, plan.widths[k])
        for part in range(0, plan.widths[k], width):
            at = plan.starts[k] + part
            b, column = at // LOW, at % LOW
            outs[k][:, part : part + width] = total[b * n : (b + 1) * n, column : column + width].astype(BF)


def own_scatter_kernel(plan, weight, grad, high, low, total, values):
    spread_values(plan, weight, grad, values)
    scatter_loop(plan, values, high, low, total, 0, plan.own_blocks)


def final_kernel(plan, place, total, face, corner, *refs):
    messages, (mine_out, theirs_out, work) = refs[: plan.slots], refs[plan.slots :]
    core, y = place[0], place[1]
    n, s = plan.channels, plan.share
    masked, hots = [], []
    for k in range(plan.slots):
        rows = plan.send_rows(k, y, face, corner)
        high = lax.shift_right_logical(rows, 8).astype(F32).astype(BF)
        hots.append(lows((rows & (LOW - 1)).astype(F32).astype(BF), LOW, plan.widths[k]))
        value = messages[k][...]
        masked.append(
            jnp.concatenate(
                [jnp.where(high == BF(b), value, BF(0)) for b in range(plan.own_blocks)], axis=0
            )
        )
    work[...] = total[...] + lax.dot_general(
        jnp.concatenate(masked, axis=1),
        jnp.concatenate(hots, axis=1),
        (((1,), (1,)), ((), ())),
        preferred_element_type=F32,
    )
    at_own = pl.multiple_of(core * s, s)
    at_other = pl.multiple_of((1 - core) * s, s)
    for b in range(plan.own_blocks):
        mine_out[:, b * LOW : (b + 1) * LOW] = work[pl.ds(b * n + at_own, s), :]
        theirs_out[:, b * LOW : (b + 1) * LOW] = work[pl.ds(b * n + at_other, s), :]


def coarse_kernel(plan, place, mine, theirs, weight, out):
    share = plan.coarse_share
    pooled = (mine[...] + theirs[...]).astype(BF)
    wide = lax.dot_general(
        weight[...], pooled, (((0,), (0,)), ((), ())), preferred_element_type=F32
    ).astype(BF)
    out[...] = jnp.where(place[0] == 0, wide[:share], wide[share:])


def sum_over(value, axis):
    count = lax.axis_size(axis)
    if count & (count - 1):
        return lax.psum(value, axis)
    distance = 1
    while distance < count:
        pairs = [(i, i ^ distance) for i in range(count)]
        value = value + lax.ppermute(value, axis, pairs)
        distance *= 2
    return value


def shards(
    fine_features,
    neighbours,
    face_send,
    corner_send,
    owner_side,
    owner_slot,
    conv_weight,
    coarse_weight,
    coarse_grad,
):
    nx, ny, nch = (lax.axis_size(a) for a in ("tx", "ty", "ch"))
    plan = Plan(
        [
            a.shape
            for a in (fine_features, neighbours, face_send, corner_send, coarse_weight, coarse_grad)
        ],
        nx,
        ny,
        nch,
    )
    n, s, half, m = plan.channels, plan.share, plan.half, plan.coarse
    swap = [(0, 1), (1, 0)]
    wide = plan.offsets * n
    bind = functools.partial
    place = jnp.stack([lax.axis_index("ch"), lax.axis_index("ty")]).astype(jnp.int32)

    other = lax.ppermute(fine_features, "ch", swap)
    tall = -(-plan.offsets // 8) * 8
    high, low, side, slot = call(
        bind(prepare_kernel, plan),
        "prepare",
        [((tall, half), F32), ((tall, half), F32), ((1, half), F32), ((1, half), F32)],
        [],
        1 << 20,
        place,
        neighbours,
        owner_side.reshape(1, -1),
        owner_slot.reshape(1, -1),
    )
    extra = plan.coarse_channels // n * m
    table, *sent = call(
        bind(pack_kernel, plan),
        "pack",
        [((plan.own_blocks * n, LOW), BF)] + [((n, w + extra), BF) for w in plan.widths],
        [],
        1 << 30,
        place,
        fine_features,
        other,
        face_send,
        corner_send,
        coarse_grad,
    )
    received = [forward(plan, k, sent[k]) for k in range(plan.slots)]
    work = 2 * wide * half * LOW
    (before,) = call(
        bind(own_gather_kernel, plan),
        "own_gather",
        [((wide, half), BF)],
        [],
        work * plan.own_blocks,
        table,
        high,
        low,
        smem=0,
    )
    weight = conv_weight.reshape(wide, n)
    owners = plan.slots + 1
    pieces = plan.coarse_share // s
    across = -(-wide // 128) * 128 + pieces * n
    grad, mine, theirs, *parts = call(
        bind(middle_kernel, plan),
        "middle",
        [((n, half), BF), ((s, across), F32), ((s, across), F32)] + [((n, m), F32)] * owners,
        [
            ((plan.halo_blocks * n, LOW), BF),
            ((wide, half), BF),
            ((plan.coarse_channels, owners * m), BF),
            ((owners * n, m), BF),
            ((n, across), F32),
            ((owners * n, m), F32),
        ],
        work * plan.halo_blocks,
        place,
        *received,
        before,
        high,
        low,
        side,
        slot,
        weight,
        coarse_weight,
        coarse_grad,
    )
    mine = mine + lax.ppermute(theirs, "ch", swap)
    returned = [backward(plan, k, parts[k + 1]) for k in range(plan.slots)]
    halo = call(
        bind(halo_scatter_kernel, plan),
        "halo_scatter",
        [((n, w), BF) for w in plan.widths],
        [((wide, half), BF), ((plan.halo_blocks * n, LOW), F32)],
        work * plan.halo_blocks,
        weight,
        grad,
        high,
        low,
        smem=0,
    )
    halo_back = [backward(plan, k, halo[k]) for k in range(plan.slots)]
    (total,) = call(
        bind(own_scatter_kernel, plan),
        "own_scatter",
        [((plan.own_blocks * n, LOW), F32)],
        [((wide, half), BF)],
        work * plan.own_blocks,
        weight,
        grad,
        high,
        low,
        smem=0,
    )
    pooled = sum(returned, parts[0])
    pooled_other = lax.ppermute(pooled, "ch", swap)
    (coarse_out,) = call(
        bind(coarse_kernel, plan),
        "coarse",
        [((plan.coarse_share, m), BF)],
        [],
        1 << 24,
        place,
        pooled,
        pooled_other,
        coarse_weight,
    )
    mine = sum_over(sum_over(mine, "ty"), "tx")
    final_mine, final_theirs = call(
        bind(final_kernel, plan),
        "final",
        [((s, plan.voxels), F32)] * 2,
        [((plan.own_blocks * n, LOW), F32)],
        1 << 30,
        place,
        total,
        face_send,
        corner_send,
        *halo_back,
    )
    input_grad = (final_mine + lax.ppermute(final_theirs, "ch", swap)).astype(BF)
    conv_weight_grad = mine[:, :wide].reshape(s, plan.offsets, n).transpose(1, 2, 0)
    coarse_part = mine[:, across - pieces * n :].reshape(s, pieces, n)
    coarse_weight_grad = coarse_part.transpose(2, 1, 0).reshape(n, plan.coarse_share)
    return (coarse_out, input_grad, conv_weight_grad, coarse_weight_grad)


def solution(mesh):
    tiles = ("group", "tx", "ty")
    in_specs = (
        P("ch", tiles),
        P(None, tiles),
        P(None, tiles),
        P(None, tiles),
        P(tiles),
        P(tiles),
        P(),
        P(),
        P(None, tiles),
    )
    out_specs = (
        P("ch", tiles),
        P("ch", tiles),
        P("group", None, "ch"),
        P("group", "ch"),
    )
    return jax.shard_map(shards, mesh=mesh, in_specs=in_specs, out_specs=out_specs, check_vma=False)
```

```python
import functools

import jax
import jax.numpy as jnp
from jax import lax
from jax.experimental import pallas as pl
from jax.experimental.pallas import tpu as pltpu
from jax.sharding import PartitionSpec as P

BF = jnp.bfloat16
F32 = jnp.float32
STEPS = ((-1, 0), (1, 0), (0, -1), (0, 1), (-1, -1), (-1, 1), (1, -1), (1, 1))
LOW = 256
VMEM_LIMIT = 56 << 20


def call(kernel, name, outs, scratch, flops, *args):
    return pl.pallas_call(
        kernel,
        name=name,
        out_shape=[jax.ShapeDtypeStruct(s, d) for s, d in outs],
        in_specs=[pl.BlockSpec(memory_space=pltpu.VMEM)] * len(args),
        out_specs=[pl.BlockSpec(memory_space=pltpu.VMEM)] * len(outs),
        scratch_shapes=[pltpu.VMEM(s, d) for s, d in scratch],
        compiler_params=pltpu.CompilerParams(vmem_limit_bytes=VMEM_LIMIT),
        cost_estimate=pl.CostEstimate(flops=flops, bytes_accessed=1 << 20, transcendentals=0),
    )(*args)


class Plan:
    def __init__(self, shapes, nx, ny, nch):
        features, neighbours, face_send, corner_send, coarse_weight, coarse_grad = shapes
        self.nx, self.ny, self.nch = nx, ny, nch
        self.share, self.voxels = features
        self.channels = self.share * nch
        self.offsets = neighbours[0]
        self.half = self.voxels // nch
        self.face, self.corner = face_send[1], corner_send[1]
        self.coarse_channels, self.coarse = coarse_grad
        self.coarse_share = self.coarse_channels // nch
        self.own_blocks = self.voxels // LOW
        self.paired = ny == 2
        self.widths = [self.face] * (3 if self.paired else 4)
        self.widths += [self.corner] * (2 if self.paired else 4)
        self.slots = len(self.widths)
        self.halo = sum(self.widths)
        self.halo_blocks = self.halo // LOW
        self.starts = [sum(self.widths[:s]) for s in range(self.slots)]
        self.nothing = self.voxels + self.halo
        self.itself = self.offsets // 2
        self.tiles = nx * ny
        self.groups = ((0, 1), (3, 4), (2, 2)) if self.paired else ((0, 1), (2, 3), (4, 5), (6, 7))
        self.swaps = sum(a != b for a, b in self.groups)
        self.early = min(2, self.half // LOW)
        self.padded = -(-self.offsets * self.channels // 128) * 128
        self.sum_width = self.padded + self.coarse_channels * self.channels // nch // self.share

    def directions(self, slot):
        if self.paired:
            return ((0,), (1,), (2, 3), (4, 5), (6, 7))[slot]
        return (slot,)

    def pairs(self, first, second):
        found = []
        for core, slot in enumerate((first, second)):
            for x in range(self.nx):
                for y in range(self.ny):
                    for d in self.directions(slot):
                        sx, sy = x + STEPS[d][0], y + STEPS[d][1]
                        if 0 <= sx < self.nx and 0 <= sy < self.ny:
                            here, there = x * self.ny + y, sx * self.ny + sy
                            found.append((there * self.nch + core, here * self.nch + core))
        return found

    def opposite(self, slot):
        return ((1, 0, 2, 4, 3) if self.paired else (1, 0, 3, 2, 7, 6, 5, 4))[slot]

    def bordering(self, slot, x, y):
        step = STEPS[self.directions(slot)[0]]
        to_x = x + step[0]
        there = (to_x >= 0) & (to_x < self.nx)
        if self.paired:
            to_y = 1 - y if step[1] else y
        else:
            to_y = y + step[1]
            there = there & (to_y >= 0) & (to_y < self.ny)
        return jnp.where(there, to_x * self.ny + to_y, -1)

    def send_rows(self, slot, y, face, corner):
        if not self.paired:
            if slot < 4:
                index = (1, 0, 3, 2)[slot]
                return face[index : index + 1, :]
            index = (3, 2, 1, 0)[slot - 4]
            return corner[index : index + 1, :]
        if slot == 0:
            return face[1:2, :]
        if slot == 1:
            return face[0:1, :]
        if slot == 2:
            return jnp.where(y == 0, face[3:4, :], face[2:3, :])
        if slot == 3:
            return jnp.where(y == 0, corner[3:4, :], corner[2:3, :])
        return jnp.where(y == 0, corner[1:2, :], corner[0:1, :])

    def rows(self, index, y):
        if not self.paired:
            return jnp.minimum(index, self.nothing)
        v, f, c = self.voxels, self.face, self.corner
        along_y = v + 2 * f
        corners = v + 4 * f
        end = corners + 4 * c
        mine = jnp.where(y == 0, along_y + f, along_y)
        of_y = jnp.where((index >= mine) & (index < mine + f), index - mine + along_y, self.nothing)
        result = jnp.where(index < along_y, index, of_y)
        first = jnp.where(y == 0, c, 0)
        at = index - corners - first
        one = jnp.where((at >= 0) & (at < c), at + v + 3 * f, self.nothing)
        two = jnp.where((at >= 2 * c) & (at < 3 * c), at - c + v + 3 * f, one)
        return jnp.where((index >= corners) & (index < end), two, result)

    def owner_slots(self, side):
        if not self.paired:
            return side
        return jnp.where(side < 3, side, jnp.where(side < 5, 3, jnp.where(side < 7, 4, 5)))


def lows(low, height, width):
    iota = lax.broadcasted_iota(jnp.int32, (height, width), 0).astype(BF)
    return jnp.where(iota == low, BF(1), BF(0))


def where_am_i(plan):
    core, x, y = (lax.axis_index(a) for a in ("ch", "tx", "ty"))
    return core, x, y


def prepare_kernel(plan, neighbours, side, slot, high_out, low_out, side_out, slot_out):
    core, _, y = where_am_i(plan)
    mine = pl.ds(pl.multiple_of(core * plan.half, plan.half), plan.half)
    rows = plan.rows(neighbours[:, mine], y)
    pad = high_out.shape[0] - plan.offsets
    fill = jnp.zeros((pad, plan.half), jnp.int32)
    rows = jnp.concatenate([rows, fill], axis=0) if pad else rows
    high_out[...] = lax.shift_right_logical(rows, 8).astype(F32)
    low_out[...] = (rows & (LOW - 1)).astype(F32)
    side_out[...] = plan.owner_slots(side[:, mine]).astype(F32)
    slot_out[...] = slot[:, mine].astype(F32)


def pack_kernel(plan, own, other, face, corner, coarse_grad, table, *messages):
    core, _, y = where_am_i(plan)
    s, n = plan.share, plan.channels
    at_own = pl.multiple_of(core * s, s)
    at_other = pl.multiple_of((1 - core) * s, s)
    for b in range(plan.own_blocks):
        table[pl.ds(b * n + at_own, s), :] = own[:, b * LOW : (b + 1) * LOW]
        table[pl.ds(b * n + at_other, s), :] = other[:, b * LOW : (b + 1) * LOW]
    groups = plan.coarse_channels // n
    for g, (first, second) in enumerate(plan.groups):
        width = plan.widths[first]
        rows = plan.send_rows(first, y, face, corner)
        if second != first:
            rows = jnp.where(core == 0, rows, plan.send_rows(second, y, face, corner))
        high = lax.shift_right_logical(rows, 8)
        hot = lows((rows & (LOW - 1)).astype(F32).astype(BF), LOW, width)
        part = jnp.dot(table[...], hot, preferred_element_type=F32)
        picked = jnp.zeros((n, width), F32)
        for b in range(plan.own_blocks):
            picked = jnp.where(high == b, part[b * n : (b + 1) * n], picked)
        messages[g][:, :width] = picked.astype(BF)
        for q in range(groups):
            at = width + q * plan.coarse
            messages[g][:, at : at + plan.coarse] = coarse_grad[q * n : (q + 1) * n, :]


def gather_block(plan, table, high_ref, low_ref, out, fs, base, blocks, before=None):
    n = plan.channels
    for k in range(plan.offsets):
        if k == plan.itself:
            continue
        at = slice(k * n, (k + 1) * n)
        low = low_ref[k : k + 1, fs].astype(BF)
        high = high_ref[k : k + 1, fs]
        part = jnp.dot(table[...], lows(low, LOW, LOW), preferred_element_type=F32)
        if before is None:
            picked = jnp.zeros((n, LOW), F32)
        else:
            picked = before[at, fs].astype(F32)
        for b in range(blocks):
            picked = jnp.where(high == float(base + b), part[b * n : (b + 1) * n], picked)
        out[at, fs] = picked.astype(BF)


def columns(block):
    return pl.ds(pl.multiple_of(block * LOW, LOW), LOW)


def own_gather_kernel(plan, table, high, low, out):
    def body(j, carry):
        gather_block(plan, table, high, low, out, columns(j), 0, plan.own_blocks)
        return carry

    lax.fori_loop(0, plan.early, body, 0)


def middle_kernel(plan, *refs):
    n, s, m = plan.channels, plan.share, plan.coarse
    count = len(plan.groups)
    received, refs = refs[:count], refs[count:]
    swapped, refs = refs[: plan.swaps], refs[plan.swaps :]
    own_table, before, high, low, side, slot, weight, coarse_weight, coarse_grad, refs = (
        *refs[:9],
        refs[9:],
    )
    grad_out, mine_out, theirs_out, table, rows, coarse_all, pooled_all, sums, parts, coarse_sum = refs
    core, _, _ = where_am_i(plan)
    messages = {}
    other = iter(swapped)
    for g, (first, second) in enumerate(plan.groups):
        here = received[g][...]
        if first == second:
            messages[first] = here
        else:
            there = next(other)[...]
            messages[first] = jnp.where(core == 0, here, there)
            messages[second] = jnp.where(core == 0, there, here)
    own = plan.own_blocks * n
    table[:own, :] = own_table[...]
    for k in range(plan.slots):
        for part in range(0, plan.widths[k], min(LOW, plan.widths[k])):
            width = min(LOW, plan.widths[k])
            at = plan.starts[k] + part
            b, column = at // LOW, at % LOW
            table[own + b * n : own + (b + 1) * n, column : column + width] = messages[k][
                :, part : part + width
            ]
    groups = plan.coarse_channels // n
    coarse_all[:, :m] = coarse_grad[...]
    for k in range(plan.slots):
        for g in range(groups):
            at = plan.widths[k] + g * m
            coarse_all[g * n : (g + 1) * n, (k + 1) * m : (k + 2) * m] = messages[k][:, at : at + m]

    def rest(j, carry):
        fs = columns(j)
        gather_block(plan, table.at[own:, :], high, low, rows, fs, plan.own_blocks, plan.halo_blocks, before)
        return carry

    def whole(j, carry):
        fs = columns(j)
        gather_block(plan, table, high, low, rows, fs, 0, plan.own_blocks + plan.halo_blocks)
        return carry

    if plan.early:
        lax.fori_loop(0, plan.early, rest, 0)
    lax.fori_loop(plan.early, plan.half // LOW, whole, 0)
    for j in range(plan.half // LOW):
        at = pl.multiple_of((core * (plan.half // LOW) + j) * n, n)
        rows[plan.itself * n : (plan.itself + 1) * n, j * LOW : (j + 1) * LOW] = table[pl.ds(at, n), :]

    grads = jnp.dot(coarse_weight[...], coarse_all[...], preferred_element_type=F32).astype(BF)
    owners = plan.slots + 1
    for k in range(owners):
        pooled_all[k * n : (k + 1) * n, :] = grads[:, k * m : (k + 1) * m]
    chunk = min(plan.half, 512)
    wide = plan.offsets * n
    sums[...] = jnp.zeros_like(sums)
    parts[...] = jnp.zeros_like(parts)
    for c in range(plan.half // chunk):
        fs = slice(c * chunk, (c + 1) * chunk)
        picked = rows[:, fs]
        hidden = lax.dot_general(
            weight[...], picked, (((0,), (0,)), ((), ())), preferred_element_type=F32
        )
        sigma = 1.0 / (1.0 + jnp.exp(-hidden))
        active = (hidden * sigma).astype(BF)
        owner = side[:, fs]
        owner_low = owner.astype(BF)
        hot = lows(slot[:, fs].astype(BF), m, chunk)
        spread = jnp.concatenate(
            [jnp.where(owner_low == BF(k), active, BF(0)) for k in range(owners)], axis=0
        )
        parts[...] += lax.dot_general(
            spread, hot, (((1,), (1,)), ((), ())), preferred_element_type=F32
        )
        found = jnp.dot(pooled_all[...], hot, preferred_element_type=F32)
        above = jnp.zeros((n, chunk), F32)
        for k in range(owners):
            above = jnp.where(owner == float(k), found[k * n : (k + 1) * n], above)
        grad = (above * (sigma * (1.0 + hidden * (1.0 - sigma)))).astype(BF)
        grad_out[:, fs] = grad
        sums[:, :wide] += lax.dot_general(
            grad, picked, (((1,), (1,)), ((), ())), preferred_element_type=F32
        )
    total = jnp.zeros((n, plan.coarse_channels), F32)
    for k in range(owners):
        value = parts[k * n : (k + 1) * n, :]
        first = value.astype(BF)
        second = (value - first.astype(F32)).astype(BF)
        grads_k = coarse_all[:, k * m : (k + 1) * m]
        for piece in (first, second):
            total = total + lax.dot_general(
                piece, grads_k, (((1,), (1,)), ((), ())), preferred_element_type=F32
            )
    for h in range(plan.nch):
        half = total[:, h * plan.coarse_share : (h + 1) * plan.coarse_share]
        for q in range(n // s):
            at = q * plan.coarse_share
            coarse_sum[h * s : (h + 1) * s, at : at + plan.coarse_share] = half[q * s : (q + 1) * s]
    at_own = pl.multiple_of(core * s, s)
    at_other = pl.multiple_of((1 - core) * s, s)
    padded = sums.shape[1]
    after = padded + coarse_sum.shape[1]
    for out, at in ((mine_out, at_own), (theirs_out, at_other)):
        out[:, :padded] = sums[pl.ds(at, s), :]
        out[:, padded:after] = coarse_sum[pl.ds(at, s), :]
        for k in range(owners):
            out[:, after + k * m : after + (k + 1) * m] = parts[pl.ds(k * n + at, s), :]


def scatter_loop(plan, values, high_ref, low_ref, total, base, blocks):
    n = plan.channels
    total[...] = jnp.zeros_like(total)

    def body(j, carry):
        fs = columns(j)
        masked, hots = [], []
        for k in range(plan.offsets):
            if k == plan.itself:
                continue
            high = high_ref[k : k + 1, fs].astype(BF)
            hots.append(lows(low_ref[k : k + 1, fs].astype(BF), LOW, LOW))
            value = values[k * n : (k + 1) * n, fs]
            masked.append(
                jnp.concatenate(
                    [jnp.where(high == BF(base + b), value, BF(0)) for b in range(blocks)], axis=0
                )
            )
        total[...] += lax.dot_general(
            jnp.concatenate(masked, axis=1),
            jnp.concatenate(hots, axis=1),
            (((1,), (1,)), ((), ())),
            preferred_element_type=F32,
        )
        return carry

    lax.fori_loop(0, plan.half // LOW, body, 0)


def spread_values(plan, weight, grad, values):
    chunk = min(plan.half, 512)
    for c in range(plan.half // chunk):
        fs = slice(c * chunk, (c + 1) * chunk)
        values[:, fs] = jnp.dot(weight[...], grad[:, fs], preferred_element_type=F32).astype(BF)


def halo_scatter_kernel(plan, weight, grad, high, low, total, values):
    spread_values(plan, weight, grad, values)
    scatter_loop(plan, values, high, low, total, plan.own_blocks, plan.halo_blocks)


def join_kernel(plan, mine, theirs, halo, joined_out, send):
    _, x, y = where_am_i(plan)
    n, s, m = plan.channels, plan.share, plan.coarse
    joined_out[...] = mine[...] + theirs[...]
    width = plan.sum_width // (n // s)
    for t in range(plan.tiles):
        for q in range(n // s):
            send[t, q * s : (q + 1) * s, :width] = joined_out[:, q * width : (q + 1) * width].astype(BF)
    part = m // (n // s)
    for k in range(plan.slots):
        tile = plan.bordering(k, x, y)

        @pl.when(tile >= 0)
        def _():
            at = plan.sum_width + (k + 1) * m
            for q in range(n // s):
                send[tile, q * s : (q + 1) * s, width : width + part] = joined_out[
                    :, at + q * part : at + (q + 1) * part
                ].astype(BF)
            size = min(LOW, plan.widths[k])
            for start in range(0, plan.widths[k], size):
                b, column = (plan.starts[k] + start) // LOW, (plan.starts[k] + start) % LOW
                to = width + part + start
                send[tile, :, to : to + size] = halo[b * n : (b + 1) * n, column : column + size].astype(BF)


def own_scatter_kernel(plan, weight, grad, high, low, total, values):
    core, _, _ = where_am_i(plan)
    n = plan.channels
    spread_values(plan, weight, grad, values)
    scatter_loop(plan, values, high, low, total, 0, plan.own_blocks)
    for j in range(plan.half // LOW):
        at = pl.ds(pl.multiple_of((core * (plan.half // LOW) + j) * n, n), n)
        total[at, :] += values[plan.itself * n : (plan.itself + 1) * n, j * LOW : (j + 1) * LOW].astype(F32)


def final_kernel(plan, total, joined, arrived, face, corner, coarse_weight, *refs):
    mine_out, theirs_out, coarse_mine, coarse_theirs, conv_out, coarse_grad_out, work, product = refs
    core, x, y = where_am_i(plan)
    n, s, m = plan.channels, plan.share, plan.coarse
    width = plan.sum_width // (n // s)
    part = m // (n // s)
    masked, hots = [], []
    pooled = joined[:, plan.sum_width : plan.sum_width + m]
    for k in range(plan.slots):
        tile = plan.bordering(k, x, y)
        there = tile >= 0
        tile = jnp.maximum(tile, 0)
        rows = plan.send_rows(plan.opposite(k), y, face, corner)
        high = lax.shift_right_logical(rows, 8).astype(F32).astype(BF)
        high = jnp.where(there, high, BF(-1))
        hots.append(lows((rows & (LOW - 1)).astype(F32).astype(BF), LOW, plan.widths[k]))
        value = arrived[tile, :, width + part : width + part + plan.widths[k]]
        masked.append(
            jnp.concatenate(
                [jnp.where(high == BF(b), value, BF(0)) for b in range(plan.own_blocks)], axis=0
            )
        )
        more = jnp.concatenate(
            [arrived[tile, q * s : (q + 1) * s, width : width + part] for q in range(n // s)], axis=1
        )
        pooled = pooled + jnp.where(there, more.astype(F32), 0.0)
    work[...] = total[...] + lax.dot_general(
        jnp.concatenate(masked, axis=1),
        jnp.concatenate(hots, axis=1),
        (((1,), (1,)), ((), ())),
        preferred_element_type=F32,
    )
    at_own = pl.multiple_of(core * s, s)
    at_other = pl.multiple_of((1 - core) * s, s)
    for b in range(plan.own_blocks):
        mine_out[:, b * LOW : (b + 1) * LOW] = work[pl.ds(b * n + at_own, s), :]
        theirs_out[:, b * LOW : (b + 1) * LOW] = work[pl.ds(b * n + at_other, s), :]
    share = plan.coarse_share
    product[...] = lax.dot_general(
        coarse_weight[pl.ds(at_own, s), :], pooled.astype(BF), (((0,), (0,)), ((), ())), preferred_element_type=F32
    )
    coarse_mine[...] = product[pl.ds(pl.multiple_of(core * share, share), share), :]
    coarse_theirs[...] = product[pl.ds(pl.multiple_of((1 - core) * share, share), share), :]
    summed = arrived[0, :, :width].astype(F32)
    for t in range(1, plan.tiles):
        summed = summed + arrived[t, :, :width].astype(F32)
    summed = jnp.concatenate([summed[q * s : (q + 1) * s] for q in range(n // s)], axis=1)
    conv_out[...] = jnp.transpose(summed)[: plan.offsets * n]
    for q in range(n // s):
        at = plan.padded + q * share
        coarse_grad_out[q * s : (q + 1) * s, :] = summed[:, at : at + share]


def add_kernel(plan, mine, theirs, coarse_mine, coarse_theirs, out, coarse_out):
    out[...] = (mine[...] + theirs[...]).astype(BF)
    coarse_out[...] = (coarse_mine[...] + coarse_theirs[...]).astype(BF)


def shards(
    fine_features,
    neighbours,
    face_send,
    corner_send,
    owner_side,
    owner_slot,
    conv_weight,
    coarse_weight,
    coarse_grad,
):
    nx, ny, nch = (lax.axis_size(a) for a in ("tx", "ty", "ch"))
    plan = Plan(
        [
            a.shape
            for a in (fine_features, neighbours, face_send, corner_send, coarse_weight, coarse_grad)
        ],
        nx,
        ny,
        nch,
    )
    n, s, half, m = plan.channels, plan.share, plan.half, plan.coarse
    wide = plan.offsets * n

    def swap(value):
        return lax.ppermute(value, "ch", [(0, 1), (1, 0)])

    def run(kernel, name, outs, scratch, flops, *args):
        return call(functools.partial(kernel, plan), name, outs, scratch, flops, *args)

    other = swap(fine_features)
    tall = -(-plan.offsets // 8) * 8
    high, low, side, slot = run(
        prepare_kernel,
        "prepare",
        [((tall, half), F32), ((tall, half), F32), ((1, half), F32), ((1, half), F32)],
        [],
        1 << 20,
        neighbours,
        owner_side.reshape(1, -1),
        owner_slot.reshape(1, -1),
    )
    extra = plan.coarse_channels // n * m
    table, *sent = run(
        pack_kernel,
        "pack",
        [((plan.own_blocks * n, LOW), BF)]
        + [((n, plan.widths[first] + extra), BF) for first, _ in plan.groups],
        [],
        1 << 30,
        fine_features,
        other,
        face_send,
        corner_send,
        coarse_grad,
    )
    received = [
        lax.ppermute(value, ("tx", "ty", "ch"), plan.pairs(first, second))
        for value, (first, second) in zip(sent, plan.groups)
    ]
    split = [g for g, (first, second) in enumerate(plan.groups) if first != second]
    early_table, *ready = lax.optimization_barrier((table, *[received[g] for g in split]))
    for g, value in zip(split, ready):
        received[g] = value
    swapped = [swap(received[g]) for g in split]
    work = 2 * wide * half * LOW
    early = plan.early * LOW
    (before,) = run(
        own_gather_kernel,
        "own_gather",
        [((wide, early), BF)],
        [],
        work * plan.own_blocks * early // half,
        early_table,
        high,
        low,
    )
    weight = conv_weight.reshape(wide, n)
    owners = plan.slots + 1
    across = plan.sum_width + owners * m
    grad, mine, theirs = run(
        middle_kernel,
        "middle",
        [((n, half), BF), ((s, across), F32), ((s, across), F32)],
        [
            (((plan.own_blocks + plan.halo_blocks) * n, LOW), BF),
            ((wide, half), BF),
            ((plan.coarse_channels, owners * m), BF),
            ((owners * n, m), BF),
            ((n, plan.padded), F32),
            ((owners * n, m), F32),
            ((n, plan.sum_width - plan.padded), F32),
        ],
        work * (plan.own_blocks + plan.halo_blocks),
        *received,
        *swapped,
        table,
        before,
        high,
        low,
        side,
        slot,
        weight,
        coarse_weight,
        coarse_grad,
    )
    theirs = swap(theirs)
    (halo,) = run(
        halo_scatter_kernel,
        "halo_scatter",
        [((plan.halo_blocks * n, LOW), F32)],
        [((wide, half), BF)],
        work * plan.halo_blocks,
        weight,
        grad,
        high,
        low,
    )
    message = plan.sum_width // (n // s) + m // (n // s) + max(plan.widths)
    joined, send = run(
        join_kernel,
        "join",
        [((s, across), F32), ((plan.tiles, n, message), BF)],
        [],
        1 << 20,
        mine,
        theirs,
        halo,
    )
    arrived = lax.all_to_all(send, ("tx", "ty"), 0, 0, tiled=True)
    (total,) = run(
        own_scatter_kernel,
        "own_scatter",
        [((plan.own_blocks * n, LOW), F32)],
        [((wide, half), BF)],
        work * plan.own_blocks,
        weight,
        grad,
        high,
        low,
    )
    share = plan.coarse_share
    mine, theirs, coarse_mine, coarse_theirs, conv_weight_grad, coarse_weight_grad = run(
        final_kernel,
        "final",
        [((s, plan.voxels), F32)] * 2 + [((share, m), F32)] * 2 + [((wide, s), F32), ((n, share), F32)],
        [((plan.own_blocks * n, LOW), F32), ((plan.coarse_channels, m), F32)],
        1 << 30,
        total,
        joined,
        arrived,
        face_send,
        corner_send,
        coarse_weight,
    )
    input_grad, coarse_out = run(
        add_kernel,
        "add",
        [((s, plan.voxels), BF), ((share, m), BF)],
        [],
        1 << 20,
        mine,
        swap(theirs),
        coarse_mine,
        swap(coarse_theirs),
    )
    return (coarse_out, input_grad, conv_weight_grad.reshape(plan.offsets, n, s), coarse_weight_grad)


def solution(mesh):
    tiles = ("group", "tx", "ty")
    in_specs = (
        P("ch", tiles),
        P(None, tiles),
        P(None, tiles),
        P(None, tiles),
        P(tiles),
        P(tiles),
        P(),
        P(),
        P(None, tiles),
    )
    out_specs = (
        P("ch", tiles),
        P("ch", tiles),
        P("group", None, "ch"),
        P("group", "ch"),
    )
    return jax.shard_map(shards, mesh=mesh, in_specs=in_specs, out_specs=out_specs, check_vma=False)
```

```python
import functools

import jax
import jax.numpy as jnp
from jax import lax
from jax.experimental import pallas as pl
from jax.experimental.pallas import tpu as pltpu
from jax.sharding import PartitionSpec as P

BF = jnp.bfloat16
F32 = jnp.float32
STEPS = ((-1, 0), (1, 0), (0, -1), (0, 1), (-1, -1), (-1, 1), (1, -1), (1, 1))
LOW = 256


def call(kernel, name, outs, scratch, flops, mib, *args):
    return pl.pallas_call(
        kernel,
        name=name,
        out_shape=[jax.ShapeDtypeStruct(s, d) for s, d in outs],
        in_specs=[pl.BlockSpec(memory_space=pltpu.VMEM)] * len(args),
        out_specs=[pl.BlockSpec(memory_space=pltpu.VMEM)] * len(outs),
        scratch_shapes=[pltpu.VMEM(s, d) for s, d in scratch],
        compiler_params=pltpu.CompilerParams(vmem_limit_bytes=mib << 20),
        cost_estimate=pl.CostEstimate(flops=flops, bytes_accessed=1 << 20, transcendentals=0),
    )(*args)


class Plan:
    def __init__(self, shapes, nx, ny, nch):
        features, neighbours, face_send, corner_send, coarse_weight, coarse_grad = shapes
        self.nx, self.ny, self.nch = nx, ny, nch
        self.share, self.voxels = features
        self.channels = self.share * nch
        self.offsets = neighbours[0]
        self.half = self.voxels // nch
        self.face, self.corner = face_send[1], corner_send[1]
        self.coarse_channels, self.coarse = coarse_grad
        self.coarse_share = self.coarse_channels // nch
        self.own_blocks = self.voxels // LOW
        self.paired = ny == 2
        self.widths = [self.face] * (3 if self.paired else 4)
        self.widths += [self.corner] * (2 if self.paired else 4)
        self.slots = len(self.widths)
        self.halo = sum(self.widths)
        self.halo_blocks = self.halo // LOW
        self.starts = [sum(self.widths[:s]) for s in range(self.slots)]
        self.nothing = self.voxels + self.halo
        self.itself = self.offsets // 2
        self.tiles = nx * ny
        self.groups = ((0, 1), (3, 4), (2, 2)) if self.paired else ((0, 1), (2, 3), (4, 5), (6, 7))
        self.swaps = sum(a != b for a, b in self.groups)
        self.early = (2, 1)
        self.padded = -(-self.offsets * self.channels // 128) * 128
        self.sum_width = self.padded + self.coarse_channels * self.channels // nch // self.share

    def directions(self, slot):
        if self.paired:
            return ((0,), (1,), (2, 3), (4, 5), (6, 7))[slot]
        return (slot,)

    def pairs(self, first, second):
        found = []
        for core, slot in enumerate((first, second)):
            for x in range(self.nx):
                for y in range(self.ny):
                    for d in self.directions(slot):
                        sx, sy = x + STEPS[d][0], y + STEPS[d][1]
                        if 0 <= sx < self.nx and 0 <= sy < self.ny:
                            here, there = x * self.ny + y, sx * self.ny + sy
                            found.append((there * self.nch + core, here * self.nch + core))
        return found

    def opposite(self, slot):
        return ((1, 0, 2, 4, 3) if self.paired else (1, 0, 3, 2, 7, 6, 5, 4))[slot]

    def bordering(self, slot, x, y):
        step = STEPS[self.directions(slot)[0]]
        to_x = x + step[0]
        there = (to_x >= 0) & (to_x < self.nx)
        if self.paired:
            to_y = 1 - y if step[1] else y
        else:
            to_y = y + step[1]
            there = there & (to_y >= 0) & (to_y < self.ny)
        return jnp.where(there, to_x * self.ny + to_y, -1)

    def send_rows(self, slot, y, face, corner):
        if not self.paired:
            if slot < 4:
                index = (1, 0, 3, 2)[slot]
                return face[index : index + 1, :]
            index = (3, 2, 1, 0)[slot - 4]
            return corner[index : index + 1, :]
        if slot == 0:
            return face[1:2, :]
        if slot == 1:
            return face[0:1, :]
        if slot == 2:
            return jnp.where(y == 0, face[3:4, :], face[2:3, :])
        if slot == 3:
            return jnp.where(y == 0, corner[3:4, :], corner[2:3, :])
        return jnp.where(y == 0, corner[1:2, :], corner[0:1, :])

    def rows(self, index, y):
        if not self.paired:
            return jnp.minimum(index, self.nothing)
        v, f, c = self.voxels, self.face, self.corner
        along_y = v + 2 * f
        corners = v + 4 * f
        end = corners + 4 * c
        mine = jnp.where(y == 0, along_y + f, along_y)
        of_y = jnp.where((index >= mine) & (index < mine + f), index - mine + along_y, self.nothing)
        result = jnp.where(index < along_y, index, of_y)
        first = jnp.where(y == 0, c, 0)
        at = index - corners - first
        one = jnp.where((at >= 0) & (at < c), at + v + 3 * f, self.nothing)
        two = jnp.where((at >= 2 * c) & (at < 3 * c), at - c + v + 3 * f, one)
        return jnp.where((index >= corners) & (index < end), two, result)

    def owner_slots(self, side):
        if not self.paired:
            return side
        return jnp.where(side < 3, side, jnp.where(side < 5, 3, jnp.where(side < 7, 4, 5)))


def lows(low, height, width):
    iota = lax.broadcasted_iota(jnp.int32, (height, width), 0).astype(BF)
    return jnp.where(iota == low, BF(1), BF(0))


def where_am_i(plan):
    core, x, y = (lax.axis_index(a) for a in ("ch", "tx", "ty"))
    return core, x, y


def prepare_kernel(plan, neighbours, side, slot, high_out, low_out, side_out, slot_out):
    core, _, y = where_am_i(plan)
    mine = pl.ds(pl.multiple_of(core * plan.half, plan.half), plan.half)
    rows = plan.rows(neighbours[:, mine], y)
    pad = high_out.shape[0] - plan.offsets
    fill = jnp.zeros((pad, plan.half), jnp.int32)
    rows = jnp.concatenate([rows, fill], axis=0) if pad else rows
    high_out[...] = lax.shift_right_logical(rows, 8).astype(F32)
    low_out[...] = (rows & (LOW - 1)).astype(F32)
    side_out[...] = plan.owner_slots(side[:, mine]).astype(F32)
    slot_out[...] = slot[:, mine].astype(F32)


def pack_kernel(plan, own, other, face, corner, coarse_grad, table, *messages):
    core, _, y = where_am_i(plan)
    s, n = plan.share, plan.channels
    at_own = pl.multiple_of(core * s, s)
    at_other = pl.multiple_of((1 - core) * s, s)
    for b in range(plan.own_blocks):
        table[pl.ds(b * n + at_own, s), :] = own[:, b * LOW : (b + 1) * LOW]
        table[pl.ds(b * n + at_other, s), :] = other[:, b * LOW : (b + 1) * LOW]
    groups = plan.coarse_channels // n
    for g, (first, second) in enumerate(plan.groups):
        width = plan.widths[first]
        rows = plan.send_rows(first, y, face, corner)
        if second != first:
            rows = jnp.where(core == 0, rows, plan.send_rows(second, y, face, corner))
        high = lax.shift_right_logical(rows, 8)
        hot = lows((rows & (LOW - 1)).astype(F32).astype(BF), LOW, width)
        part = jnp.dot(table[...], hot, preferred_element_type=F32)
        picked = jnp.zeros((n, width), F32)
        for b in range(plan.own_blocks):
            picked = jnp.where(high == b, part[b * n : (b + 1) * n], picked)
        messages[g][:, :width] = picked.astype(BF)
        for q in range(groups):
            at = width + q * plan.coarse
            messages[g][:, at : at + plan.coarse] = coarse_grad[q * n : (q + 1) * n, :]


def gather_block(plan, table, high_ref, low_ref, out, fs, base, blocks, to=None, before=None):
    to = fs if to is None else to
    n = plan.channels
    for k in range(plan.offsets):
        if k == plan.itself:
            continue
        at = slice(k * n, (k + 1) * n)
        low = low_ref[k : k + 1, fs].astype(BF)
        high = high_ref[k : k + 1, fs]
        part = jnp.dot(table[...], lows(low, LOW, LOW), preferred_element_type=F32)
        if before is None:
            picked = jnp.zeros((n, LOW), F32)
        else:
            picked = before[at, to].astype(F32)
        for b in range(blocks):
            picked = jnp.where(high == float(base + b), part[b * n : (b + 1) * n], picked)
        out[at, fs if before is not None else to] = picked.astype(BF)


def columns(block):
    return pl.ds(pl.multiple_of(block * LOW, LOW), LOW)


def own_gather_kernel(plan, first, count, table, high, low, out):
    n = plan.channels

    def body(j, carry):
        gather_block(plan, table, high, low, out, columns(first + j), 0, plan.own_blocks, columns(j))
        return carry

    lax.fori_loop(0, count, body, 0)


def middle_kernel(plan, *refs):
    n, s, m = plan.channels, plan.share, plan.coarse
    count = len(plan.groups)
    received, refs = refs[:count], refs[count:]
    swapped, refs = refs[: plan.swaps], refs[plan.swaps :]
    befores, refs = refs[: len(plan.early)], refs[len(plan.early) :]
    own_table, high, low, side, slot, weight, coarse_weight, coarse_grad, refs = (*refs[:8], refs[8:])
    grad_out, mine_out, theirs_out, table, rows, coarse_all, pooled_all, sums, parts, coarse_sum = refs
    core, _, _ = where_am_i(plan)
    messages = {}
    other = iter(swapped)
    for g, (first, second) in enumerate(plan.groups):
        here = received[g][...]
        if first == second:
            messages[first] = here
        else:
            there = next(other)[...]
            messages[first] = jnp.where(core == 0, here, there)
            messages[second] = jnp.where(core == 0, there, here)
    own = plan.own_blocks * n
    table[:own, :] = own_table[...]
    for k in range(plan.slots):
        for part in range(0, plan.widths[k], min(LOW, plan.widths[k])):
            width = min(LOW, plan.widths[k])
            at = plan.starts[k] + part
            b, column = at // LOW, at % LOW
            table[own + b * n : own + (b + 1) * n, column : column + width] = messages[k][
                :, part : part + width
            ]
    groups = plan.coarse_channels // n
    coarse_all[:, :m] = coarse_grad[...]
    for k in range(plan.slots):
        for g in range(groups):
            at = plan.widths[k] + g * m
            coarse_all[g * n : (g + 1) * n, (k + 1) * m : (k + 2) * m] = messages[k][:, at : at + m]

    def whole(j, carry):
        gather_block(plan, table, high, low, rows, columns(j), 0, plan.own_blocks + plan.halo_blocks)
        return carry

    done = 0
    halo_table = table.at[own:, :]
    for before, count in zip(befores, plan.early):

        def rest(j, carry):
            gather_block(
                plan,
                halo_table,
                high,
                low,
                rows,
                columns(done + j),
                plan.own_blocks,
                plan.halo_blocks,
                columns(j),
                before,
            )
            return carry

        lax.fori_loop(0, count, rest, 0)
        done += count
    lax.fori_loop(done, plan.half // LOW, whole, 0)
    for j in range(plan.half // LOW):
        at = pl.multiple_of((core * (plan.half // LOW) + j) * n, n)
        rows[plan.itself * n : (plan.itself + 1) * n, j * LOW : (j + 1) * LOW] = table[pl.ds(at, n), :]

    grads = jnp.dot(coarse_weight[...], coarse_all[...], preferred_element_type=F32).astype(BF)
    owners = plan.slots + 1
    for k in range(owners):
        pooled_all[k * n : (k + 1) * n, :] = grads[:, k * m : (k + 1) * m]
    chunk = min(plan.half, 512)
    wide = plan.offsets * n
    sums[...] = jnp.zeros_like(sums)
    parts[...] = jnp.zeros_like(parts)
    for c in range(plan.half // chunk):
        fs = slice(c * chunk, (c + 1) * chunk)
        picked = rows[:, fs]
        hidden = lax.dot_general(
            weight[...], picked, (((0,), (0,)), ((), ())), preferred_element_type=F32
        )
        sigma = 1.0 / (1.0 + jnp.exp(-hidden))
        active = (hidden * sigma).astype(BF)
        owner = side[:, fs]
        owner_low = owner.astype(BF)
        hot = lows(slot[:, fs].astype(BF), m, chunk)
        spread = jnp.concatenate(
            [jnp.where(owner_low == BF(k), active, BF(0)) for k in range(owners)], axis=0
        )
        parts[...] += lax.dot_general(
            spread, hot, (((1,), (1,)), ((), ())), preferred_element_type=F32
        )
        found = jnp.dot(pooled_all[...], hot, preferred_element_type=F32)
        above = jnp.zeros((n, chunk), F32)
        for k in range(owners):
            above = jnp.where(owner == float(k), found[k * n : (k + 1) * n], above)
        grad = (above * (sigma * (1.0 + hidden * (1.0 - sigma)))).astype(BF)
        grad_out[:, fs] = grad
        sums[:, :wide] += lax.dot_general(
            grad, picked, (((1,), (1,)), ((), ())), preferred_element_type=F32
        )
    total = jnp.zeros((n, plan.coarse_channels), F32)
    for k in range(owners):
        value = parts[k * n : (k + 1) * n, :]
        first = value.astype(BF)
        second = (value - first.astype(F32)).astype(BF)
        grads_k = coarse_all[:, k * m : (k + 1) * m]
        for piece in (first, second):
            total = total + lax.dot_general(
                piece, grads_k, (((1,), (1,)), ((), ())), preferred_element_type=F32
            )
    for h in range(plan.nch):
        half = total[:, h * plan.coarse_share : (h + 1) * plan.coarse_share]
        for q in range(n // s):
            at = q * plan.coarse_share
            coarse_sum[h * s : (h + 1) * s, at : at + plan.coarse_share] = half[q * s : (q + 1) * s]
    at_own = pl.multiple_of(core * s, s)
    at_other = pl.multiple_of((1 - core) * s, s)
    padded = sums.shape[1]
    after = padded + coarse_sum.shape[1]
    for out, at in ((mine_out, at_own), (theirs_out, at_other)):
        out[:, :padded] = sums[pl.ds(at, s), :]
        out[:, padded:after] = coarse_sum[pl.ds(at, s), :]
        for k in range(owners):
            out[:, after + k * m : after + (k + 1) * m] = parts[pl.ds(k * n + at, s), :]


def scatter_loop(plan, values, high_ref, low_ref, total, base, blocks):
    n = plan.channels
    total[...] = jnp.zeros_like(total)

    width = min(plan.half, 2 * LOW)

    def body(j, carry):
        fs = pl.ds(pl.multiple_of(j * width, width), width)
        masked, hots = [], []
        for k in range(plan.offsets):
            if k == plan.itself:
                continue
            high = high_ref[k : k + 1, fs].astype(BF)
            hots.append(lows(low_ref[k : k + 1, fs].astype(BF), LOW, width))
            value = values[k * n : (k + 1) * n, fs]
            masked.append(
                jnp.concatenate(
                    [jnp.where(high == BF(base + b), value, BF(0)) for b in range(blocks)], axis=0
                )
            )
        total[...] += lax.dot_general(
            jnp.concatenate(masked, axis=1),
            jnp.concatenate(hots, axis=1),
            (((1,), (1,)), ((), ())),
            preferred_element_type=F32,
        )
        return carry

    lax.fori_loop(0, plan.half // width, body, 0)


def spread_values(plan, weight, grad, values):
    chunk = min(plan.half, 512)
    for c in range(plan.half // chunk):
        fs = slice(c * chunk, (c + 1) * chunk)
        values[:, fs] = jnp.dot(weight[...], grad[:, fs], preferred_element_type=F32).astype(BF)


def halo_scatter_kernel(plan, weight, grad, high, low, total, values):
    spread_values(plan, weight, grad, values)
    scatter_loop(plan, values, high, low, total, plan.own_blocks, plan.halo_blocks)


def join_kernel(plan, mine, theirs, halo, joined_out, send):
    _, x, y = where_am_i(plan)
    n, s, m = plan.channels, plan.share, plan.coarse
    joined_out[...] = mine[...] + theirs[...]
    width = plan.sum_width // (n // s)
    for t in range(plan.tiles):
        for q in range(n // s):
            send[t, q * s : (q + 1) * s, :width] = joined_out[:, q * width : (q + 1) * width].astype(BF)
    part = m // (n // s)
    for k in range(plan.slots):
        tile = plan.bordering(k, x, y)

        @pl.when(tile >= 0)
        def _():
            at = plan.sum_width + (k + 1) * m
            for q in range(n // s):
                send[tile, q * s : (q + 1) * s, width : width + part] = joined_out[
                    :, at + q * part : at + (q + 1) * part
                ].astype(BF)
            size = min(LOW, plan.widths[k])
            for start in range(0, plan.widths[k], size):
                b, column = (plan.starts[k] + start) // LOW, (plan.starts[k] + start) % LOW
                to = width + part + start
                send[tile, :, to : to + size] = halo[b * n : (b + 1) * n, column : column + size].astype(BF)


def own_scatter_kernel(plan, weight, grad, high, low, total, values):
    core, _, _ = where_am_i(plan)
    n = plan.channels
    spread_values(plan, weight, grad, values)
    scatter_loop(plan, values, high, low, total, 0, plan.own_blocks)
    for j in range(plan.half // LOW):
        at = pl.ds(pl.multiple_of((core * (plan.half // LOW) + j) * n, n), n)
        total[at, :] += values[plan.itself * n : (plan.itself + 1) * n, j * LOW : (j + 1) * LOW].astype(F32)


def final_kernel(plan, total, joined, arrived, face, corner, coarse_weight, *refs):
    mine_out, theirs_out, coarse_mine, coarse_theirs, conv_out, coarse_grad_out, work, product = refs
    core, x, y = where_am_i(plan)
    n, s, m = plan.channels, plan.share, plan.coarse
    width = plan.sum_width // (n // s)
    part = m // (n // s)
    masked, hots = [], []
    pooled = joined[:, plan.sum_width : plan.sum_width + m]
    for k in range(plan.slots):
        tile = plan.bordering(k, x, y)
        there = tile >= 0
        tile = jnp.maximum(tile, 0)
        rows = plan.send_rows(plan.opposite(k), y, face, corner)
        high = lax.shift_right_logical(rows, 8).astype(F32).astype(BF)
        high = jnp.where(there, high, BF(-1))
        hots.append(lows((rows & (LOW - 1)).astype(F32).astype(BF), LOW, plan.widths[k]))
        value = arrived[tile, :, width + part : width + part + plan.widths[k]]
        masked.append(
            jnp.concatenate(
                [jnp.where(high == BF(b), value, BF(0)) for b in range(plan.own_blocks)], axis=0
            )
        )
        more = jnp.concatenate(
            [arrived[tile, q * s : (q + 1) * s, width : width + part] for q in range(n // s)], axis=1
        )
        pooled = pooled + jnp.where(there, more.astype(F32), 0.0)
    work[...] = total[...] + lax.dot_general(
        jnp.concatenate(masked, axis=1),
        jnp.concatenate(hots, axis=1),
        (((1,), (1,)), ((), ())),
        preferred_element_type=F32,
    )
    at_own = pl.multiple_of(core * s, s)
    at_other = pl.multiple_of((1 - core) * s, s)
    for b in range(plan.own_blocks):
        mine_out[:, b * LOW : (b + 1) * LOW] = work[pl.ds(b * n + at_own, s), :]
        theirs_out[:, b * LOW : (b + 1) * LOW] = work[pl.ds(b * n + at_other, s), :]
    share = plan.coarse_share
    product[...] = lax.dot_general(
        coarse_weight[pl.ds(at_own, s), :], pooled.astype(BF), (((0,), (0,)), ((), ())), preferred_element_type=F32
    )
    coarse_mine[...] = product[pl.ds(pl.multiple_of(core * share, share), share), :]
    coarse_theirs[...] = product[pl.ds(pl.multiple_of((1 - core) * share, share), share), :]
    summed = arrived[0, :, :width].astype(F32)
    for t in range(1, plan.tiles):
        summed = summed + arrived[t, :, :width].astype(F32)
    summed = jnp.concatenate([summed[q * s : (q + 1) * s] for q in range(n // s)], axis=1)
    for k in range(plan.offsets):
        conv_out[k] = summed[:, k * n : (k + 1) * n]
    for q in range(n // s):
        at = plan.padded + q * share
        coarse_grad_out[q * s : (q + 1) * s, :] = summed[:, at : at + share]


def add_kernel(plan, mine, theirs, coarse_mine, coarse_theirs, out, coarse_out):
    out[...] = (mine[...] + theirs[...]).astype(BF)
    coarse_out[...] = (coarse_mine[...] + coarse_theirs[...]).astype(BF)


def shards(
    fine_features,
    neighbours,
    face_send,
    corner_send,
    owner_side,
    owner_slot,
    conv_weight,
    coarse_weight,
    coarse_grad,
):
    nx, ny, nch = (lax.axis_size(a) for a in ("tx", "ty", "ch"))
    plan = Plan(
        [
            a.shape
            for a in (fine_features, neighbours, face_send, corner_send, coarse_weight, coarse_grad)
        ],
        nx,
        ny,
        nch,
    )
    n, s, half, m = plan.channels, plan.share, plan.half, plan.coarse
    wide = plan.offsets * n

    def swap(value):
        return lax.ppermute(value, "ch", [(0, 1), (1, 0)])

    def run(kernel, name, outs, scratch, flops, mib, *args):
        return call(functools.partial(kernel, plan), name, outs, scratch, flops, mib, *args)

    other = swap(fine_features)
    tall = -(-plan.offsets // 8) * 8
    high, low, side, slot = run(
        prepare_kernel,
        "prepare",
        [((tall, half), F32), ((tall, half), F32), ((1, half), F32), ((1, half), F32)],
        [],
        1 << 20,
        6,
        neighbours,
        owner_side.reshape(1, -1),
        owner_slot.reshape(1, -1),
    )
    extra = plan.coarse_channels // n * m
    own, side = lax.optimization_barrier((fine_features, side))
    table, *sent = run(
        pack_kernel,
        "pack",
        [((plan.own_blocks * n, LOW), BF)]
        + [((n, plan.widths[first] + extra), BF) for first, _ in plan.groups],
        [],
        1 << 30,
        6,
        own,
        other,
        face_send,
        corner_send,
        coarse_grad,
    )
    received = [
        lax.ppermute(value, ("tx", "ty", "ch"), plan.pairs(first, second))
        for value, (first, second) in zip(sent, plan.groups)
    ]
    split = [g for g, (first, second) in enumerate(plan.groups) if first != second]
    work = 2 * wide * half * LOW
    befores = []
    early_table, first = table, 0
    for step, count in enumerate(plan.early):
        (before,) = call(
            functools.partial(own_gather_kernel, plan, first, count),
            "own_gather",
            [((wide, count * LOW), BF)],
            [],
            work * plan.own_blocks * count * LOW // half,
            16,
            early_table,
            high,
            low,
        )
        befores.append(before)
        first += count
        if step == 0:
            early_table, before, *ready = lax.optimization_barrier(
                (table, before, *[received[g] for g in split])
            )
            befores[0] = before
            for g, value in zip(split, ready):
                received[g] = value
            swapped = [swap(received[g]) for g in split]
    weight = conv_weight.reshape(wide, n)
    owners = plan.slots + 1
    across = plan.sum_width + owners * m
    grad, mine, theirs = run(
        middle_kernel,
        "middle",
        [((n, half), BF), ((s, across), F32), ((s, across), F32)],
        [
            (((plan.own_blocks + plan.halo_blocks) * n, LOW), BF),
            ((wide, half), BF),
            ((plan.coarse_channels, owners * m), BF),
            ((owners * n, m), BF),
            ((n, plan.padded), F32),
            ((owners * n, m), F32),
            ((n, plan.sum_width - plan.padded), F32),
        ],
        work * (plan.own_blocks + plan.halo_blocks),
        24,
        *received,
        *swapped,
        *befores,
        table,
        high,
        low,
        side,
        slot,
        weight,
        coarse_weight,
        coarse_grad,
    )
    theirs = swap(theirs)
    (halo,) = run(
        halo_scatter_kernel,
        "halo_scatter",
        [((plan.halo_blocks * n, LOW), F32)],
        [((wide, half), BF)],
        work * plan.halo_blocks,
        16,
        weight,
        grad,
        high,
        low,
    )
    message = plan.sum_width // (n // s) + m // (n // s) + max(plan.widths)
    joined, send = run(
        join_kernel,
        "join",
        [((s, across), F32), ((plan.tiles, n, message), BF)],
        [],
        1 << 20,
        6,
        mine,
        theirs,
        halo,
    )
    arrived = lax.all_to_all(send, ("tx", "ty"), 0, 0, tiled=True)
    (total,) = run(
        own_scatter_kernel,
        "own_scatter",
        [((plan.own_blocks * n, LOW), F32)],
        [((wide, half), BF)],
        work * plan.own_blocks,
        16,
        weight,
        grad,
        high,
        low,
    )
    share = plan.coarse_share
    mine, theirs, coarse_mine, coarse_theirs, conv_weight_grad, coarse_weight_grad = run(
        final_kernel,
        "final",
        [((s, plan.voxels), F32)] * 2 + [((share, m), F32)] * 2 + [((plan.offsets, s, n), F32), ((n, share), F32)],
        [((plan.own_blocks * n, LOW), F32), ((plan.coarse_channels, m), F32)],
        1 << 30,
        12,
        total,
        joined,
        arrived,
        face_send,
        corner_send,
        coarse_weight,
    )
    input_grad, coarse_out = run(
        add_kernel,
        "add",
        [((s, plan.voxels), BF), ((share, m), BF)],
        [],
        1 << 20,
        6,
        mine,
        swap(theirs),
        coarse_mine,
        swap(coarse_theirs),
    )
    return (coarse_out, input_grad, conv_weight_grad.transpose(0, 2, 1), coarse_weight_grad)


def solution(mesh):
    tiles = ("group", "tx", "ty")
    in_specs = (
        P("ch", tiles),
        P(None, tiles),
        P(None, tiles),
        P(None, tiles),
        P(tiles),
        P(tiles),
        P(),
        P(),
        P(None, tiles),
    )
    out_specs = (
        P("ch", tiles),
        P("ch", tiles),
        P("group", None, "ch"),
        P("group", "ch"),
    )
    return jax.shard_map(shards, mesh=mesh, in_specs=in_specs, out_specs=out_specs, check_vma=False)
```

```python
import functools

import jax
import jax.numpy as jnp
from jax import lax
from jax.experimental import pallas as pl
from jax.experimental.pallas import tpu as pltpu
from jax.sharding import PartitionSpec as P

BF = jnp.bfloat16
F32 = jnp.float32
STEPS = ((-1, 0), (1, 0), (0, -1), (0, 1), (-1, -1), (-1, 1), (1, -1), (1, 1))
LOW = 256


def call(kernel, name, outs, scratch, flops, mib, *args):
    return pl.pallas_call(
        kernel,
        name=name,
        out_shape=[jax.ShapeDtypeStruct(s, d) for s, d in outs],
        in_specs=[pl.BlockSpec(memory_space=pltpu.VMEM)] * len(args),
        out_specs=[pl.BlockSpec(memory_space=pltpu.VMEM)] * len(outs),
        scratch_shapes=[pltpu.VMEM(s, d) for s, d in scratch],
        compiler_params=pltpu.CompilerParams(vmem_limit_bytes=mib << 20),
        cost_estimate=pl.CostEstimate(flops=flops, bytes_accessed=1 << 20, transcendentals=0),
    )(*args)


class Plan:
    def __init__(self, shapes, nx, ny, nch):
        features, neighbours, face_send, corner_send, coarse_weight, coarse_grad = shapes
        self.nx, self.ny, self.nch = nx, ny, nch
        self.share, self.voxels = features
        self.channels = self.share * nch
        self.offsets = neighbours[0]
        self.half = self.voxels // nch
        self.face, self.corner = face_send[1], corner_send[1]
        self.coarse_channels, self.coarse = coarse_grad
        self.coarse_share = self.coarse_channels // nch
        self.own_blocks = self.voxels // LOW
        self.paired = ny == 2
        self.widths = [self.face] * (3 if self.paired else 4)
        self.widths += [self.corner] * (2 if self.paired else 4)
        self.slots = len(self.widths)
        self.halo = sum(self.widths)
        self.halo_blocks = self.halo // LOW
        self.starts = [sum(self.widths[:s]) for s in range(self.slots)]
        self.nothing = self.voxels + self.halo
        self.wrapped = self.paired and nx % 2 == 0
        self.itself = self.offsets // 2
        self.tiles = nx * ny
        self.groups = ((0, 1), (3, 4), (2, 2)) if self.paired else ((0, 1), (2, 3), (4, 5), (6, 7))
        self.swaps = sum(a != b for a, b in self.groups)
        self.early = (2, 1)
        self.padded = -(-self.offsets * self.channels // 128) * 128
        self.sum_width = self.padded + self.coarse_channels * self.channels // nch // self.share

    def directions(self, slot):
        if self.paired:
            return ((0,), (1,), (2, 3), (4, 5), (6, 7))[slot]
        return (slot,)

    def is_first(self, core, x):
        return (core + x) % 2 == 1 if self.paired else core == 0

    def pairs(self, first, second):
        found = []
        for core in range(self.nch):
            for x in range(self.nx):
                for y in range(self.ny):
                    for d in self.directions(first if self.is_first(core, x) else second):
                        sx, sy = x + STEPS[d][0], y + STEPS[d][1]
                        if self.wrapped:
                            sx %= self.nx
                        if 0 <= sx < self.nx and 0 <= sy < self.ny:
                            here, there = x * self.ny + y, sx * self.ny + sy
                            found.append((there * self.nch + core, here * self.nch + core))
        return found

    def sent_first(self, core, x):
        return jnp.logical_not(self.is_first(core, x)) if self.paired else self.is_first(core, x)

    def opposite(self, slot):
        return ((1, 0, 2, 4, 3) if self.paired else (1, 0, 3, 2, 7, 6, 5, 4))[slot]

    def bordering(self, slot, x, y):
        step = STEPS[self.directions(slot)[0]]
        to_x = x + step[0]
        there = (to_x >= 0) & (to_x < self.nx)
        if self.paired:
            to_y = 1 - y if step[1] else y
        else:
            to_y = y + step[1]
            there = there & (to_y >= 0) & (to_y < self.ny)
        return jnp.where(there, to_x * self.ny + to_y, -1)

    def send_rows(self, slot, y, face, corner):
        if not self.paired:
            if slot < 4:
                index = (1, 0, 3, 2)[slot]
                return face[index : index + 1, :]
            index = (3, 2, 1, 0)[slot - 4]
            return corner[index : index + 1, :]
        if slot == 0:
            return face[1:2, :]
        if slot == 1:
            return face[0:1, :]
        if slot == 2:
            return jnp.where(y == 0, face[3:4, :], face[2:3, :])
        if slot == 3:
            return jnp.where(y == 0, corner[3:4, :], corner[2:3, :])
        return jnp.where(y == 0, corner[1:2, :], corner[0:1, :])

    def rows(self, index, y):
        if not self.paired:
            return jnp.minimum(index, self.nothing)
        v, f, c = self.voxels, self.face, self.corner
        along_y = v + 2 * f
        corners = v + 4 * f
        end = corners + 4 * c
        mine = jnp.where(y == 0, along_y + f, along_y)
        of_y = jnp.where((index >= mine) & (index < mine + f), index - mine + along_y, self.nothing)
        result = jnp.where(index < along_y, index, of_y)
        first = jnp.where(y == 0, c, 0)
        at = index - corners - first
        one = jnp.where((at >= 0) & (at < c), at + v + 3 * f, self.nothing)
        two = jnp.where((at >= 2 * c) & (at < 3 * c), at - c + v + 3 * f, one)
        return jnp.where((index >= corners) & (index < end), two, result)

    def owner_slots(self, side):
        if not self.paired:
            return side
        return jnp.where(side < 3, side, jnp.where(side < 5, 3, jnp.where(side < 7, 4, 5)))


def lows(low, height, width):
    iota = lax.broadcasted_iota(jnp.int32, (height, width), 0).astype(BF)
    return jnp.where(iota == low, BF(1), BF(0))


def where_am_i(plan):
    core, x, y = (lax.axis_index(a) for a in ("ch", "tx", "ty"))
    return core, x, y


def prepare_kernel(plan, neighbours, high_out, low_out):
    core, _, y = where_am_i(plan)
    mine = pl.ds(pl.multiple_of(core * plan.half, plan.half), plan.half)
    rows = plan.rows(neighbours[:, mine], y)
    pad = high_out.shape[0] - plan.offsets
    fill = jnp.zeros((pad, plan.half), jnp.int32)
    rows = jnp.concatenate([rows, fill], axis=0) if pad else rows
    high_out[...] = lax.shift_right_logical(rows, 8).astype(F32)
    low_out[...] = (rows & (LOW - 1)).astype(F32)


def pack_kernel(plan, own, other, face, corner, coarse_grad, table, *messages):
    core, x, y = where_am_i(plan)
    s, n = plan.share, plan.channels
    at_own = pl.multiple_of(core * s, s)
    at_other = pl.multiple_of((1 - core) * s, s)
    for b in range(plan.own_blocks):
        table[pl.ds(b * n + at_own, s), :] = own[:, b * LOW : (b + 1) * LOW]
        table[pl.ds(b * n + at_other, s), :] = other[:, b * LOW : (b + 1) * LOW]
    groups = plan.coarse_channels // n
    for g, (first, second) in enumerate(plan.groups):
        width = plan.widths[first]
        rows = plan.send_rows(first, y, face, corner)
        if second != first:
            rows = jnp.where(plan.sent_first(core, x), rows, plan.send_rows(second, y, face, corner))
        high = lax.shift_right_logical(rows, 8)
        hot = lows((rows & (LOW - 1)).astype(F32).astype(BF), LOW, width)
        part = jnp.dot(table[...], hot, preferred_element_type=F32)
        picked = jnp.zeros((n, width), F32)
        for b in range(plan.own_blocks):
            picked = jnp.where(high == b, part[b * n : (b + 1) * n], picked)
        messages[g][:, :width] = picked.astype(BF)
        for q in range(groups):
            at = width + q * plan.coarse
            messages[g][:, at : at + plan.coarse] = coarse_grad[q * n : (q + 1) * n, :]


def gather_block(plan, table, high_ref, low_ref, out, fs, base, blocks, to=None, before=None):
    to = fs if to is None else to
    n = plan.channels
    for k in range(plan.offsets):
        if k == plan.itself:
            continue
        at = slice(k * n, (k + 1) * n)
        low = low_ref[k : k + 1, fs].astype(BF)
        high = high_ref[k : k + 1, fs]
        part = jnp.dot(table[...], lows(low, LOW, LOW), preferred_element_type=F32)
        if before is None:
            picked = jnp.zeros((n, LOW), F32)
        else:
            picked = before[at, to].astype(F32)
        for b in range(blocks):
            picked = jnp.where(high == float(base + b), part[b * n : (b + 1) * n], picked)
        out[at, fs if before is not None else to] = picked.astype(BF)


def columns(block):
    return pl.ds(pl.multiple_of(block * LOW, LOW), LOW)


def own_gather_kernel(plan, first, count, table, high, low, out):
    n = plan.channels

    def body(j, carry):
        gather_block(plan, table, high, low, out, columns(first + j), 0, plan.own_blocks, columns(j))
        return carry

    lax.fori_loop(0, count, body, 0)


def middle_kernel(plan, *refs):
    n, s, m = plan.channels, plan.share, plan.coarse
    count = len(plan.groups)
    received, refs = refs[:count], refs[count:]
    swapped, refs = refs[: plan.swaps], refs[plan.swaps :]
    befores, refs = refs[: len(plan.early)], refs[len(plan.early) :]
    own_table, high, low, side, slot, weight, coarse_weight, coarse_grad, refs = (*refs[:8], refs[8:])
    grad_out, mine_out, theirs_out, table, rows, coarse_all, pooled_all, sums, parts, coarse_sum = refs
    core, x, y = where_am_i(plan)
    is_first = plan.is_first(core, x)
    messages = {}
    other = iter(swapped)
    for g, (first, second) in enumerate(plan.groups):
        here = received[g][...]
        if first == second:
            messages[first] = here
        else:
            there = next(other)[...]
            messages[first] = jnp.where(is_first, here, there)
            messages[second] = jnp.where(is_first, there, here)
    if plan.wrapped:
        for k in range(plan.slots):
            here = messages[k]
            messages[k] = jnp.where(plan.bordering(k, x, y) >= 0, here, jnp.zeros_like(here))
    own = plan.own_blocks * n
    table[:own, :] = own_table[...]
    for k in range(plan.slots):
        for part in range(0, plan.widths[k], min(LOW, plan.widths[k])):
            width = min(LOW, plan.widths[k])
            at = plan.starts[k] + part
            b, column = at // LOW, at % LOW
            table[own + b * n : own + (b + 1) * n, column : column + width] = messages[k][
                :, part : part + width
            ]
    groups = plan.coarse_channels // n
    coarse_all[:, :m] = coarse_grad[...]
    for k in range(plan.slots):
        for g in range(groups):
            at = plan.widths[k] + g * m
            coarse_all[g * n : (g + 1) * n, (k + 1) * m : (k + 2) * m] = messages[k][:, at : at + m]

    def whole(j, carry):
        gather_block(plan, table, high, low, rows, columns(j), 0, plan.own_blocks + plan.halo_blocks)
        return carry

    done = 0
    halo_table = table.at[own:, :]
    for before, count in zip(befores, plan.early):

        def rest(j, carry):
            gather_block(
                plan,
                halo_table,
                high,
                low,
                rows,
                columns(done + j),
                plan.own_blocks,
                plan.halo_blocks,
                columns(j),
                before,
            )
            return carry

        lax.fori_loop(0, count, rest, 0)
        done += count
    lax.fori_loop(done, plan.half // LOW, whole, 0)
    for j in range(plan.half // LOW):
        at = pl.multiple_of((core * (plan.half // LOW) + j) * n, n)
        rows[plan.itself * n : (plan.itself + 1) * n, j * LOW : (j + 1) * LOW] = table[pl.ds(at, n), :]

    grads = jnp.dot(coarse_weight[...], coarse_all[...], preferred_element_type=F32).astype(BF)
    owners = plan.slots + 1
    for k in range(owners):
        pooled_all[k * n : (k + 1) * n, :] = grads[:, k * m : (k + 1) * m]
    chunk = min(plan.half, 512)
    wide = plan.offsets * n
    sums[...] = jnp.zeros_like(sums)
    parts[...] = jnp.zeros_like(parts)
    for c in range(plan.half // chunk):
        fs = slice(c * chunk, (c + 1) * chunk)
        picked = rows[:, fs]
        hidden = lax.dot_general(
            weight[...], picked, (((0,), (0,)), ((), ())), preferred_element_type=F32
        )
        sigma = 1.0 / (1.0 + jnp.exp(-hidden))
        active = (hidden * sigma).astype(BF)
        mine = pl.ds(pl.multiple_of(core * plan.half + c * chunk, LOW), chunk)
        owner = plan.owner_slots(side[:, mine]).astype(F32)
        owner_low = owner.astype(BF)
        hot = lows(slot[:, mine].astype(F32).astype(BF), m, chunk)
        spread = jnp.concatenate(
            [jnp.where(owner_low == BF(k), active, BF(0)) for k in range(owners)], axis=0
        )
        parts[...] += lax.dot_general(
            spread, hot, (((1,), (1,)), ((), ())), preferred_element_type=F32
        )
        found = jnp.dot(pooled_all[...], hot, preferred_element_type=F32)
        above = jnp.zeros((n, chunk), F32)
        for k in range(owners):
            above = jnp.where(owner == float(k), found[k * n : (k + 1) * n], above)
        grad = (above * (sigma * (1.0 + hidden * (1.0 - sigma)))).astype(BF)
        grad_out[:, fs] = grad
        sums[:, :wide] += lax.dot_general(
            grad, picked, (((1,), (1,)), ((), ())), preferred_element_type=F32
        )
    total = jnp.zeros((n, plan.coarse_channels), F32)
    for k in range(owners):
        value = parts[k * n : (k + 1) * n, :]
        first = value.astype(BF)
        second = (value - first.astype(F32)).astype(BF)
        grads_k = coarse_all[:, k * m : (k + 1) * m]
        for piece in (first, second):
            total = total + lax.dot_general(
                piece, grads_k, (((1,), (1,)), ((), ())), preferred_element_type=F32
            )
    for h in range(plan.nch):
        half = total[:, h * plan.coarse_share : (h + 1) * plan.coarse_share]
        for q in range(n // s):
            at = q * plan.coarse_share
            coarse_sum[h * s : (h + 1) * s, at : at + plan.coarse_share] = half[q * s : (q + 1) * s]
    at_own = pl.multiple_of(core * s, s)
    at_other = pl.multiple_of((1 - core) * s, s)
    padded = sums.shape[1]
    after = padded + coarse_sum.shape[1]
    for out, at in ((mine_out, at_own), (theirs_out, at_other)):
        out[:, :padded] = sums[pl.ds(at, s), :]
        out[:, padded:after] = coarse_sum[pl.ds(at, s), :]
        for k in range(owners):
            out[:, after + k * m : after + (k + 1) * m] = parts[pl.ds(k * n + at, s), :]


def scatter_loop(plan, values, high_ref, low_ref, total, base, blocks):
    n = plan.channels
    total[...] = jnp.zeros_like(total)

    width = min(plan.half, 2 * LOW)

    def body(j, carry):
        fs = pl.ds(pl.multiple_of(j * width, width), width)
        masked, hots = [], []
        for k in range(plan.offsets):
            if k == plan.itself:
                continue
            high = high_ref[k : k + 1, fs].astype(BF)
            hots.append(lows(low_ref[k : k + 1, fs].astype(BF), LOW, width))
            value = values[k * n : (k + 1) * n, fs]
            masked.append(
                jnp.concatenate(
                    [jnp.where(high == BF(base + b), value, BF(0)) for b in range(blocks)], axis=0
                )
            )
        total[...] += lax.dot_general(
            jnp.concatenate(masked, axis=1),
            jnp.concatenate(hots, axis=1),
            (((1,), (1,)), ((), ())),
            preferred_element_type=F32,
        )
        return carry

    lax.fori_loop(0, plan.half // width, body, 0)


def spread_values(plan, weight, grad, values):
    chunk = min(plan.half, 512)
    for c in range(plan.half // chunk):
        fs = slice(c * chunk, (c + 1) * chunk)
        values[:, fs] = jnp.dot(weight[...], grad[:, fs], preferred_element_type=F32).astype(BF)


def halo_scatter_kernel(plan, weight, grad, high, low, total, values):
    spread_values(plan, weight, grad, values)
    scatter_loop(plan, values, high, low, total, plan.own_blocks, plan.halo_blocks)


def join_kernel(plan, mine, theirs, halo, joined_out, send):
    _, x, y = where_am_i(plan)
    n, s, m = plan.channels, plan.share, plan.coarse
    joined_out[...] = mine[...] + theirs[...]
    width = plan.sum_width // (n // s)
    for t in range(plan.tiles):
        for q in range(n // s):
            send[t, q * s : (q + 1) * s, :width] = joined_out[:, q * width : (q + 1) * width].astype(BF)
    part = m // (n // s)
    for k in range(plan.slots):
        tile = plan.bordering(k, x, y)

        @pl.when(tile >= 0)
        def _():
            at = plan.sum_width + (k + 1) * m
            for q in range(n // s):
                send[tile, q * s : (q + 1) * s, width : width + part] = joined_out[
                    :, at + q * part : at + (q + 1) * part
                ].astype(BF)
            size = min(LOW, plan.widths[k])
            for start in range(0, plan.widths[k], size):
                b, column = (plan.starts[k] + start) // LOW, (plan.starts[k] + start) % LOW
                to = width + part + start
                send[tile, :, to : to + size] = halo[b * n : (b + 1) * n, column : column + size].astype(BF)


def own_scatter_kernel(plan, weight, grad, high, low, total, values):
    core, _, _ = where_am_i(plan)
    n = plan.channels
    spread_values(plan, weight, grad, values)
    scatter_loop(plan, values, high, low, total, 0, plan.own_blocks)
    for j in range(plan.half // LOW):
        at = pl.ds(pl.multiple_of((core * (plan.half // LOW) + j) * n, n), n)
        total[at, :] += values[plan.itself * n : (plan.itself + 1) * n, j * LOW : (j + 1) * LOW].astype(F32)


def final_kernel(plan, total, joined, arrived, face, corner, coarse_weight, *refs):
    mine_out, theirs_out, coarse_mine, coarse_theirs, conv_out, coarse_grad_out, work, product = refs
    core, x, y = where_am_i(plan)
    n, s, m = plan.channels, plan.share, plan.coarse
    width = plan.sum_width // (n // s)
    part = m // (n // s)
    masked, hots = [], []
    pooled = joined[:, plan.sum_width : plan.sum_width + m]
    for k in range(plan.slots):
        tile = plan.bordering(k, x, y)
        there = tile >= 0
        tile = jnp.maximum(tile, 0)
        rows = plan.send_rows(plan.opposite(k), y, face, corner)
        high = lax.shift_right_logical(rows, 8).astype(F32).astype(BF)
        high = jnp.where(there, high, BF(-1))
        hots.append(lows((rows & (LOW - 1)).astype(F32).astype(BF), LOW, plan.widths[k]))
        value = arrived[tile, :, width + part : width + part + plan.widths[k]]
        masked.append(
            jnp.concatenate(
                [jnp.where(high == BF(b), value, BF(0)) for b in range(plan.own_blocks)], axis=0
            )
        )
        more = jnp.concatenate(
            [arrived[tile, q * s : (q + 1) * s, width : width + part] for q in range(n // s)], axis=1
        )
        pooled = pooled + jnp.where(there, more.astype(F32), 0.0)
    work[...] = total[...] + lax.dot_general(
        jnp.concatenate(masked, axis=1),
        jnp.concatenate(hots, axis=1),
        (((1,), (1,)), ((), ())),
        preferred_element_type=F32,
    )
    at_own = pl.multiple_of(core * s, s)
    at_other = pl.multiple_of((1 - core) * s, s)
    for b in range(plan.own_blocks):
        mine_out[:, b * LOW : (b + 1) * LOW] = work[pl.ds(b * n + at_own, s), :]
        theirs_out[:, b * LOW : (b + 1) * LOW] = work[pl.ds(b * n + at_other, s), :]
    share = plan.coarse_share
    product[...] = lax.dot_general(
        coarse_weight[pl.ds(at_own, s), :], pooled.astype(BF), (((0,), (0,)), ((), ())), preferred_element_type=F32
    )
    coarse_mine[...] = product[pl.ds(pl.multiple_of(core * share, share), share), :]
    coarse_theirs[...] = product[pl.ds(pl.multiple_of((1 - core) * share, share), share), :]
    summed = arrived[0, :, :width].astype(F32)
    for t in range(1, plan.tiles):
        summed = summed + arrived[t, :, :width].astype(F32)
    summed = jnp.concatenate([summed[q * s : (q + 1) * s] for q in range(n // s)], axis=1)
    for k in range(plan.offsets):
        conv_out[k] = summed[:, k * n : (k + 1) * n]
    for q in range(n // s):
        at = plan.padded + q * share
        coarse_grad_out[q * s : (q + 1) * s, :] = summed[:, at : at + share]


def add_kernel(plan, mine, theirs, coarse_mine, coarse_theirs, out, coarse_out):
    out[...] = (mine[...] + theirs[...]).astype(BF)
    coarse_out[...] = (coarse_mine[...] + coarse_theirs[...]).astype(BF)


def shards(
    fine_features,
    neighbours,
    face_send,
    corner_send,
    owner_side,
    owner_slot,
    conv_weight,
    coarse_weight,
    coarse_grad,
):
    nx, ny, nch = (lax.axis_size(a) for a in ("tx", "ty", "ch"))
    plan = Plan(
        [
            a.shape
            for a in (fine_features, neighbours, face_send, corner_send, coarse_weight, coarse_grad)
        ],
        nx,
        ny,
        nch,
    )
    n, s, half, m = plan.channels, plan.share, plan.half, plan.coarse
    wide = plan.offsets * n

    def swap(value):
        return lax.ppermute(value, "ch", [(0, 1), (1, 0)])

    def run(kernel, name, outs, scratch, flops, mib, *args):
        return call(functools.partial(kernel, plan), name, outs, scratch, flops, mib, *args)

    other = swap(fine_features)
    tall = -(-plan.offsets // 8) * 8
    high, low = run(
        prepare_kernel,
        "prepare",
        [((tall, half), F32), ((tall, half), F32)],
        [],
        1 << 20,
        6,
        neighbours,
    )
    extra = plan.coarse_channels // n * m
    table, *sent = run(
        pack_kernel,
        "pack",
        [((plan.own_blocks * n, LOW), BF)]
        + [((n, plan.widths[first] + extra), BF) for first, _ in plan.groups],
        [],
        1 << 30,
        6,
        fine_features,
        other,
        face_send,
        corner_send,
        coarse_grad,
    )
    received = [
        lax.ppermute(value, ("tx", "ty", "ch"), plan.pairs(first, second))
        for value, (first, second) in zip(sent, plan.groups)
    ]
    split = [g for g, (first, second) in enumerate(plan.groups) if first != second]
    work = 2 * wide * half * LOW
    befores = []
    early_table, first = table, 0
    for step, count in enumerate(plan.early):
        (before,) = call(
            functools.partial(own_gather_kernel, plan, first, count),
            "own_gather",
            [((wide, count * LOW), BF)],
            [],
            work * plan.own_blocks * count * LOW // half,
            16,
            early_table,
            high,
            low,
        )
        befores.append(before)
        first += count
        if step == 0:
            early_table, before, *ready = lax.optimization_barrier(
                (table, before, *[received[g] for g in split])
            )
            befores[0] = before
            for g, value in zip(split, ready):
                received[g] = value
            swapped = [swap(received[g]) for g in split]
    weight = conv_weight.reshape(wide, n)
    owners = plan.slots + 1
    across = plan.sum_width + owners * m
    grad, mine, theirs = run(
        middle_kernel,
        "middle",
        [((n, half), BF), ((s, across), F32), ((s, across), F32)],
        [
            (((plan.own_blocks + plan.halo_blocks) * n, LOW), BF),
            ((wide, half), BF),
            ((plan.coarse_channels, owners * m), BF),
            ((owners * n, m), BF),
            ((n, plan.padded), F32),
            ((owners * n, m), F32),
            ((n, plan.sum_width - plan.padded), F32),
        ],
        work * (plan.own_blocks + plan.halo_blocks),
        24,
        *received,
        *swapped,
        *befores,
        table,
        high,
        low,
        owner_side.reshape(1, -1),
        owner_slot.reshape(1, -1),
        weight,
        coarse_weight,
        coarse_grad,
    )
    theirs = swap(theirs)
    (halo,) = run(
        halo_scatter_kernel,
        "halo_scatter",
        [((plan.halo_blocks * n, LOW), F32)],
        [((wide, half), BF)],
        work * plan.halo_blocks,
        16,
        weight,
        grad,
        high,
        low,
    )
    message = plan.sum_width // (n // s) + m // (n // s) + max(plan.widths)
    joined, send = run(
        join_kernel,
        "join",
        [((s, across), F32), ((plan.tiles, n, message), BF)],
        [],
        1 << 20,
        6,
        mine,
        theirs,
        halo,
    )
    arrived = lax.all_to_all(send, ("tx", "ty"), 0, 0, tiled=True)
    (total,) = run(
        own_scatter_kernel,
        "own_scatter",
        [((plan.own_blocks * n, LOW), F32)],
        [((wide, half), BF)],
        work * plan.own_blocks,
        16,
        weight,
        grad,
        high,
        low,
    )
    share = plan.coarse_share
    mine, theirs, coarse_mine, coarse_theirs, conv_weight_grad, coarse_weight_grad = run(
        final_kernel,
        "final",
        [((s, plan.voxels), F32)] * 2 + [((share, m), F32)] * 2 + [((plan.offsets, s, n), F32), ((n, share), F32)],
        [((plan.own_blocks * n, LOW), F32), ((plan.coarse_channels, m), F32)],
        1 << 30,
        12,
        total,
        joined,
        arrived,
        face_send,
        corner_send,
        coarse_weight,
    )
    input_grad, coarse_out = run(
        add_kernel,
        "add",
        [((s, plan.voxels), BF), ((share, m), BF)],
        [],
        1 << 20,
        6,
        mine,
        swap(theirs),
        coarse_mine,
        swap(coarse_theirs),
    )
    return (coarse_out, input_grad, conv_weight_grad.transpose(0, 2, 1), coarse_weight_grad)


def solution(mesh):
    tiles = ("group", "tx", "ty")
    in_specs = (
        P("ch", tiles),
        P(None, tiles),
        P(None, tiles),
        P(None, tiles),
        P(tiles),
        P(tiles),
        P(),
        P(),
        P(None, tiles),
    )
    out_specs = (
        P("ch", tiles),
        P("ch", tiles),
        P("group", None, "ch"),
        P("group", "ch"),
    )
    return jax.shard_map(shards, mesh=mesh, in_specs=in_specs, out_specs=out_specs, check_vma=False)
```

```python
import functools

import jax
import jax.numpy as jnp
from jax import lax
from jax.experimental import pallas as pl
from jax.experimental.pallas import tpu as pltpu
from jax.sharding import PartitionSpec as P

BF = jnp.bfloat16
F32 = jnp.float32
STEPS = ((-1, 0), (1, 0), (0, -1), (0, 1), (-1, -1), (-1, 1), (1, -1), (1, 1))
LOW = 256


def call(kernel, name, outs, scratch, flops, mib, *args):
    return pl.pallas_call(
        kernel,
        name=name,
        out_shape=[jax.ShapeDtypeStruct(s, d) for s, d in outs],
        in_specs=[pl.BlockSpec(memory_space=pltpu.VMEM)] * len(args),
        out_specs=[pl.BlockSpec(memory_space=pltpu.VMEM)] * len(outs),
        scratch_shapes=[pltpu.VMEM(s, d) for s, d in scratch],
        compiler_params=pltpu.CompilerParams(vmem_limit_bytes=mib << 20),
        cost_estimate=pl.CostEstimate(flops=flops, bytes_accessed=1 << 20, transcendentals=0),
    )(*args)


class Plan:
    def __init__(self, shapes, nx, ny, nch):
        features, neighbours, face_send, corner_send, coarse_weight, coarse_grad = shapes
        self.nx, self.ny, self.nch = nx, ny, nch
        self.share, self.voxels = features
        self.channels = self.share * nch
        self.offsets = neighbours[0]
        self.half = self.voxels // nch
        self.face, self.corner = face_send[1], corner_send[1]
        self.coarse_channels, self.coarse = coarse_grad
        self.coarse_share = self.coarse_channels // nch
        self.own_blocks = self.voxels // LOW
        self.paired = ny == 2
        self.widths = [self.face] * (3 if self.paired else 4)
        self.widths += [self.corner] * (2 if self.paired else 4)
        self.slots = len(self.widths)
        self.halo = sum(self.widths)
        self.halo_blocks = self.halo // LOW
        self.starts = [sum(self.widths[:s]) for s in range(self.slots)]
        self.nothing = self.voxels + self.halo
        self.wrapped = self.paired and nx % 2 == 0
        self.itself = self.offsets // 2
        self.tiles = nx * ny
        self.groups = ((0, 1), (3, 4), (2, 2)) if self.paired else ((0, 1), (2, 3), (4, 5), (6, 7))
        self.swaps = sum(a != b for a, b in self.groups)
        self.early = (2, 1)
        self.padded = -(-self.offsets * self.channels // 128) * 128
        self.sum_width = self.padded + self.coarse_channels * self.channels // nch // self.share

    def directions(self, slot):
        if self.paired:
            return ((0,), (1,), (2, 3), (4, 5), (6, 7))[slot]
        return (slot,)

    def is_first(self, core, x):
        return (core + x) % 2 == 1 if self.paired else core == 0

    def pairs(self, first, second):
        found = []
        for core in range(self.nch):
            for x in range(self.nx):
                for y in range(self.ny):
                    for d in self.directions(first if self.is_first(core, x) else second):
                        sx, sy = x + STEPS[d][0], y + STEPS[d][1]
                        if self.wrapped:
                            sx %= self.nx
                        if 0 <= sx < self.nx and 0 <= sy < self.ny:
                            here, there = x * self.ny + y, sx * self.ny + sy
                            found.append((there * self.nch + core, here * self.nch + core))
        return found

    def sent_first(self, core, x):
        return jnp.logical_not(self.is_first(core, x)) if self.paired else self.is_first(core, x)

    def opposite(self, slot):
        return ((1, 0, 2, 4, 3) if self.paired else (1, 0, 3, 2, 7, 6, 5, 4))[slot]

    def bordering(self, slot, x, y):
        step = STEPS[self.directions(slot)[0]]
        to_x = x + step[0]
        there = (to_x >= 0) & (to_x < self.nx)
        if self.paired:
            to_y = 1 - y if step[1] else y
        else:
            to_y = y + step[1]
            there = there & (to_y >= 0) & (to_y < self.ny)
        return jnp.where(there, to_x * self.ny + to_y, -1)

    def send_rows(self, slot, y, face, corner):
        if not self.paired:
            if slot < 4:
                index = (1, 0, 3, 2)[slot]
                return face[index : index + 1, :]
            index = (3, 2, 1, 0)[slot - 4]
            return corner[index : index + 1, :]
        if slot == 0:
            return face[1:2, :]
        if slot == 1:
            return face[0:1, :]
        if slot == 2:
            return jnp.where(y == 0, face[3:4, :], face[2:3, :])
        if slot == 3:
            return jnp.where(y == 0, corner[3:4, :], corner[2:3, :])
        return jnp.where(y == 0, corner[1:2, :], corner[0:1, :])

    def rows(self, index, y):
        if not self.paired:
            return jnp.minimum(index, self.nothing)
        v, f, c = self.voxels, self.face, self.corner
        along_y = v + 2 * f
        corners = v + 4 * f
        end = corners + 4 * c
        mine = jnp.where(y == 0, along_y + f, along_y)
        of_y = jnp.where((index >= mine) & (index < mine + f), index - mine + along_y, self.nothing)
        result = jnp.where(index < along_y, index, of_y)
        first = jnp.where(y == 0, c, 0)
        at = index - corners - first
        one = jnp.where((at >= 0) & (at < c), at + v + 3 * f, self.nothing)
        two = jnp.where((at >= 2 * c) & (at < 3 * c), at - c + v + 3 * f, one)
        return jnp.where((index >= corners) & (index < end), two, result)

    def owner_slots(self, side):
        if not self.paired:
            return side
        return jnp.where(side < 3, side, jnp.where(side < 5, 3, jnp.where(side < 7, 4, 5)))


def lows(low, height, width):
    iota = lax.broadcasted_iota(jnp.int32, (height, width), 0).astype(BF)
    return jnp.where(iota == low, BF(1), BF(0))


def where_am_i(plan):
    core, x, y = (lax.axis_index(a) for a in ("ch", "tx", "ty"))
    return core, x, y


def prepare_kernel(plan, neighbours, high_out, low_out):
    core, _, y = where_am_i(plan)
    mine = pl.ds(pl.multiple_of(core * plan.half, plan.half), plan.half)
    rows = plan.rows(neighbours[:, mine], y)
    pad = high_out.shape[0] - plan.offsets
    fill = jnp.zeros((pad, plan.half), jnp.int32)
    rows = jnp.concatenate([rows, fill], axis=0) if pad else rows
    high_out[...] = lax.shift_right_logical(rows, 8).astype(F32)
    low_out[...] = (rows & (LOW - 1)).astype(F32)


def pack_kernel(plan, own, other, face, corner, coarse_grad, table, *messages):
    core, x, y = where_am_i(plan)
    s, n = plan.share, plan.channels
    at_own = pl.multiple_of(core * s, s)
    at_other = pl.multiple_of((1 - core) * s, s)
    for b in range(plan.own_blocks):
        table[pl.ds(b * n + at_own, s), :] = own[:, b * LOW : (b + 1) * LOW]
        table[pl.ds(b * n + at_other, s), :] = other[:, b * LOW : (b + 1) * LOW]
    groups = plan.coarse_channels // n
    for g, (first, second) in enumerate(plan.groups):
        width = plan.widths[first]
        rows = plan.send_rows(first, y, face, corner)
        if second != first:
            rows = jnp.where(plan.sent_first(core, x), rows, plan.send_rows(second, y, face, corner))
        high = lax.shift_right_logical(rows, 8)
        hot = lows((rows & (LOW - 1)).astype(F32).astype(BF), LOW, width)
        part = jnp.dot(table[...], hot, preferred_element_type=F32)
        picked = jnp.zeros((n, width), F32)
        for b in range(plan.own_blocks):
            picked = jnp.where(high == b, part[b * n : (b + 1) * n], picked)
        messages[g][:, :width] = picked.astype(BF)
        for q in range(groups):
            at = width + q * plan.coarse
            messages[g][:, at : at + plan.coarse] = coarse_grad[q * n : (q + 1) * n, :]


def gather_block(plan, table, high_ref, low_ref, out, fs, base, blocks, to=None, before=None):
    to = fs if to is None else to
    n = plan.channels
    for k in range(plan.offsets):
        if k == plan.itself:
            continue
        at = slice(k * n, (k + 1) * n)
        low = low_ref[k : k + 1, fs].astype(BF)
        high = high_ref[k : k + 1, fs]
        part = jnp.dot(table[...], lows(low, LOW, LOW), preferred_element_type=F32)
        if before is None:
            picked = jnp.zeros((n, LOW), F32)
        else:
            picked = before[at, to].astype(F32)
        for b in range(blocks):
            picked = jnp.where(high == float(base + b), part[b * n : (b + 1) * n], picked)
        out[at, fs if before is not None else to] = picked.astype(BF)


def columns(block):
    if isinstance(block, int):
        return slice(block * LOW, (block + 1) * LOW)
    return pl.ds(pl.multiple_of(block * LOW, LOW), LOW)


def blocks_loop(first, last, body):
    pairs = (last - first) // 2

    def two(j, carry):
        body(first + 2 * j)
        body(first + 2 * j + 1)
        return carry

    if pairs > 1:
        lax.fori_loop(0, pairs, two, 0)
    elif pairs:
        two(0, 0)
    if (last - first) % 2:
        body(last - 1)


def own_gather_kernel(plan, first, count, table, high, low, out):
    def body(j):
        to = columns(j - first)
        gather_block(plan, table, high, low, out, columns(j), 0, plan.own_blocks, to)

    blocks_loop(first, first + count, body)


def middle_kernel(plan, *refs):
    n, s, m = plan.channels, plan.share, plan.coarse
    count = len(plan.groups)
    received, refs = refs[:count], refs[count:]
    swapped, refs = refs[: plan.swaps], refs[plan.swaps :]
    befores, refs = refs[: len(plan.early)], refs[len(plan.early) :]
    own_table, high, low, side, slot, weight, coarse_weight, coarse_grad, refs = (*refs[:8], refs[8:])
    grad_out, mine_out, theirs_out, table, rows, coarse_all, pooled_all, sums, parts, coarse_sum = refs
    core, x, y = where_am_i(plan)
    is_first = plan.is_first(core, x)
    messages = {}
    other = iter(swapped)
    for g, (first, second) in enumerate(plan.groups):
        here = received[g][...]
        if first == second:
            messages[first] = here
        else:
            there = next(other)[...]
            messages[first] = jnp.where(is_first, here, there)
            messages[second] = jnp.where(is_first, there, here)
    if plan.wrapped:
        for k in range(plan.slots):
            here = messages[k]
            messages[k] = jnp.where(plan.bordering(k, x, y) >= 0, here, jnp.zeros_like(here))
    own = plan.own_blocks * n
    table[:own, :] = own_table[...]
    for k in range(plan.slots):
        for part in range(0, plan.widths[k], min(LOW, plan.widths[k])):
            width = min(LOW, plan.widths[k])
            at = plan.starts[k] + part
            b, column = at // LOW, at % LOW
            table[own + b * n : own + (b + 1) * n, column : column + width] = messages[k][
                :, part : part + width
            ]
    groups = plan.coarse_channels // n
    coarse_all[:, :m] = coarse_grad[...]
    for k in range(plan.slots):
        for g in range(groups):
            at = plan.widths[k] + g * m
            coarse_all[g * n : (g + 1) * n, (k + 1) * m : (k + 2) * m] = messages[k][:, at : at + m]

    halo_table = table.at[own:, :]
    done = 0
    for before, count in zip(befores, plan.early):

        def rest(j):
            of = columns(j - done)
            gather_block(
                plan, halo_table, high, low, rows, columns(j), plan.own_blocks, plan.halo_blocks, of, before
            )

        blocks_loop(done, done + count, rest)
        done += count

    def whole(j):
        gather_block(plan, table, high, low, rows, columns(j), 0, plan.own_blocks + plan.halo_blocks)

    blocks_loop(done, plan.half // LOW, whole)
    for j in range(plan.half // LOW):
        at = pl.multiple_of((core * (plan.half // LOW) + j) * n, n)
        rows[plan.itself * n : (plan.itself + 1) * n, j * LOW : (j + 1) * LOW] = table[pl.ds(at, n), :]

    grads = jnp.dot(coarse_weight[...], coarse_all[...], preferred_element_type=F32).astype(BF)
    owners = plan.slots + 1
    for k in range(owners):
        pooled_all[k * n : (k + 1) * n, :] = grads[:, k * m : (k + 1) * m]
    chunk = min(plan.half, 1024)
    wide = plan.offsets * n
    sums[...] = jnp.zeros_like(sums)
    parts[...] = jnp.zeros_like(parts)
    for c in range(plan.half // chunk):
        fs = slice(c * chunk, (c + 1) * chunk)
        picked = rows[:, fs]
        hidden = lax.dot_general(
            weight[...], picked, (((0,), (0,)), ((), ())), preferred_element_type=F32
        )
        sigma = 1.0 / (1.0 + jnp.exp(-hidden))
        active = (hidden * sigma).astype(BF)
        mine = pl.ds(pl.multiple_of(core * plan.half + c * chunk, LOW), chunk)
        owner = plan.owner_slots(side[:, mine]).astype(F32)
        owner_low = owner.astype(BF)
        hot = lows(slot[:, mine].astype(F32).astype(BF), m, chunk)
        spread = jnp.concatenate(
            [jnp.where(owner_low == BF(k), active, BF(0)) for k in range(owners)], axis=0
        )
        parts[...] += lax.dot_general(
            spread, hot, (((1,), (1,)), ((), ())), preferred_element_type=F32
        )
        found = jnp.dot(pooled_all[...], hot, preferred_element_type=F32)
        above = jnp.zeros((n, chunk), F32)
        for k in range(owners):
            above = jnp.where(owner == float(k), found[k * n : (k + 1) * n], above)
        grad = (above * (sigma * (1.0 + hidden * (1.0 - sigma)))).astype(BF)
        grad_out[:, fs] = grad
        sums[:, :wide] += lax.dot_general(
            grad, picked, (((1,), (1,)), ((), ())), preferred_element_type=F32
        )
    total = jnp.zeros((n, plan.coarse_channels), F32)
    for k in range(owners):
        value = parts[k * n : (k + 1) * n, :]
        first = value.astype(BF)
        second = (value - first.astype(F32)).astype(BF)
        grads_k = coarse_all[:, k * m : (k + 1) * m]
        for piece in (first, second):
            total = total + lax.dot_general(
                piece, grads_k, (((1,), (1,)), ((), ())), preferred_element_type=F32
            )
    for h in range(plan.nch):
        half = total[:, h * plan.coarse_share : (h + 1) * plan.coarse_share]
        for q in range(n // s):
            at = q * plan.coarse_share
            coarse_sum[h * s : (h + 1) * s, at : at + plan.coarse_share] = half[q * s : (q + 1) * s]
    at_own = pl.multiple_of(core * s, s)
    at_other = pl.multiple_of((1 - core) * s, s)
    padded = sums.shape[1]
    after = padded + coarse_sum.shape[1]
    for out, at in ((mine_out, at_own), (theirs_out, at_other)):
        out[:, :padded] = sums[pl.ds(at, s), :]
        out[:, padded:after] = coarse_sum[pl.ds(at, s), :]
        for k in range(owners):
            out[:, after + k * m : after + (k + 1) * m] = parts[pl.ds(k * n + at, s), :]


def scatter_loop(plan, values, high_ref, low_ref, total, base, blocks):
    n = plan.channels
    total[...] = jnp.zeros_like(total)

    width = min(plan.half, 2 * LOW)

    def body(j, carry):
        fs = pl.ds(pl.multiple_of(j * width, width), width)
        masked, hots = [], []
        for k in range(plan.offsets):
            if k == plan.itself:
                continue
            high = high_ref[k : k + 1, fs].astype(BF)
            hots.append(lows(low_ref[k : k + 1, fs].astype(BF), LOW, width))
            value = values[k * n : (k + 1) * n, fs]
            masked.append(
                jnp.concatenate(
                    [jnp.where(high == BF(base + b), value, BF(0)) for b in range(blocks)], axis=0
                )
            )
        total[...] += lax.dot_general(
            jnp.concatenate(masked, axis=1),
            jnp.concatenate(hots, axis=1),
            (((1,), (1,)), ((), ())),
            preferred_element_type=F32,
        )
        return carry

    lax.fori_loop(0, plan.half // width, body, 0)


def spread_values(plan, weight, grad, values):
    chunk = min(plan.half, 512)
    for c in range(plan.half // chunk):
        fs = slice(c * chunk, (c + 1) * chunk)
        values[:, fs] = jnp.dot(weight[...], grad[:, fs], preferred_element_type=F32).astype(BF)


def halo_scatter_kernel(plan, weight, grad, high, low, total, values):
    spread_values(plan, weight, grad, values)
    scatter_loop(plan, values, high, low, total, plan.own_blocks, plan.halo_blocks)


def join_kernel(plan, mine, theirs, halo, joined_out, send):
    _, x, y = where_am_i(plan)
    n, s, m = plan.channels, plan.share, plan.coarse
    joined_out[...] = mine[...] + theirs[...]
    width = plan.sum_width // (n // s)
    for t in range(plan.tiles):
        for q in range(n // s):
            send[t, q * s : (q + 1) * s, :width] = joined_out[:, q * width : (q + 1) * width].astype(BF)
    part = m // (n // s)
    for k in range(plan.slots):
        tile = plan.bordering(k, x, y)

        @pl.when(tile >= 0)
        def _():
            at = plan.sum_width + (k + 1) * m
            for q in range(n // s):
                send[tile, q * s : (q + 1) * s, width : width + part] = joined_out[
                    :, at + q * part : at + (q + 1) * part
                ].astype(BF)
            size = min(LOW, plan.widths[k])
            for start in range(0, plan.widths[k], size):
                b, column = (plan.starts[k] + start) // LOW, (plan.starts[k] + start) % LOW
                to = width + part + start
                send[tile, :, to : to + size] = halo[b * n : (b + 1) * n, column : column + size].astype(BF)


def own_scatter_kernel(plan, weight, grad, high, low, total, values):
    core, _, _ = where_am_i(plan)
    n = plan.channels
    spread_values(plan, weight, grad, values)
    scatter_loop(plan, values, high, low, total, 0, plan.own_blocks)
    for j in range(plan.half // LOW):
        at = pl.ds(pl.multiple_of((core * (plan.half // LOW) + j) * n, n), n)
        total[at, :] += values[plan.itself * n : (plan.itself + 1) * n, j * LOW : (j + 1) * LOW].astype(F32)


def final_kernel(plan, total, joined, arrived, face, corner, coarse_weight, *refs):
    mine_out, theirs_out, coarse_mine, coarse_theirs, conv_out, coarse_grad_out, work, product = refs
    core, x, y = where_am_i(plan)
    n, s, m = plan.channels, plan.share, plan.coarse
    width = plan.sum_width // (n // s)
    part = m // (n // s)
    masked, hots = [], []
    pooled = joined[:, plan.sum_width : plan.sum_width + m]
    for k in range(plan.slots):
        tile = plan.bordering(k, x, y)
        there = tile >= 0
        tile = jnp.maximum(tile, 0)
        rows = plan.send_rows(plan.opposite(k), y, face, corner)
        high = lax.shift_right_logical(rows, 8).astype(F32).astype(BF)
        high = jnp.where(there, high, BF(-1))
        hots.append(lows((rows & (LOW - 1)).astype(F32).astype(BF), LOW, plan.widths[k]))
        value = arrived[tile, :, width + part : width + part + plan.widths[k]]
        masked.append(
            jnp.concatenate(
                [jnp.where(high == BF(b), value, BF(0)) for b in range(plan.own_blocks)], axis=0
            )
        )
        more = jnp.concatenate(
            [arrived[tile, q * s : (q + 1) * s, width : width + part] for q in range(n // s)], axis=1
        )
        pooled = pooled + jnp.where(there, more.astype(F32), 0.0)
    work[...] = total[...] + lax.dot_general(
        jnp.concatenate(masked, axis=1),
        jnp.concatenate(hots, axis=1),
        (((1,), (1,)), ((), ())),
        preferred_element_type=F32,
    )
    at_own = pl.multiple_of(core * s, s)
    at_other = pl.multiple_of((1 - core) * s, s)
    for b in range(plan.own_blocks):
        mine_out[:, b * LOW : (b + 1) * LOW] = work[pl.ds(b * n + at_own, s), :]
        theirs_out[:, b * LOW : (b + 1) * LOW] = work[pl.ds(b * n + at_other, s), :]
    share = plan.coarse_share
    product[...] = lax.dot_general(
        coarse_weight[pl.ds(at_own, s), :], pooled.astype(BF), (((0,), (0,)), ((), ())), preferred_element_type=F32
    )
    coarse_mine[...] = product[pl.ds(pl.multiple_of(core * share, share), share), :]
    coarse_theirs[...] = product[pl.ds(pl.multiple_of((1 - core) * share, share), share), :]
    summed = arrived[0, :, :width].astype(F32)
    for t in range(1, plan.tiles):
        summed = summed + arrived[t, :, :width].astype(F32)
    summed = jnp.concatenate([summed[q * s : (q + 1) * s] for q in range(n // s)], axis=1)
    for k in range(plan.offsets):
        conv_out[k] = summed[:, k * n : (k + 1) * n]
    for q in range(n // s):
        at = plan.padded + q * share
        coarse_grad_out[q * s : (q + 1) * s, :] = summed[:, at : at + share]


def add_kernel(plan, mine, theirs, coarse_mine, coarse_theirs, out, coarse_out):
    out[...] = (mine[...] + theirs[...]).astype(BF)
    coarse_out[...] = (coarse_mine[...] + coarse_theirs[...]).astype(BF)


def shards(
    fine_features,
    neighbours,
    face_send,
    corner_send,
    owner_side,
    owner_slot,
    conv_weight,
    coarse_weight,
    coarse_grad,
):
    nx, ny, nch = (lax.axis_size(a) for a in ("tx", "ty", "ch"))
    plan = Plan(
        [
            a.shape
            for a in (fine_features, neighbours, face_send, corner_send, coarse_weight, coarse_grad)
        ],
        nx,
        ny,
        nch,
    )
    n, s, half, m = plan.channels, plan.share, plan.half, plan.coarse
    wide = plan.offsets * n

    def swap(value):
        return lax.ppermute(value, "ch", [(0, 1), (1, 0)])

    def run(kernel, name, outs, scratch, flops, mib, *args):
        return call(functools.partial(kernel, plan), name, outs, scratch, flops, mib, *args)

    other = swap(fine_features)
    tall = -(-plan.offsets // 8) * 8
    high, low = run(
        prepare_kernel,
        "prepare",
        [((tall, half), F32), ((tall, half), F32)],
        [],
        1 << 20,
        6,
        neighbours,
    )
    extra = plan.coarse_channels // n * m
    table, *sent = run(
        pack_kernel,
        "pack",
        [((plan.own_blocks * n, LOW), BF)]
        + [((n, plan.widths[first] + extra), BF) for first, _ in plan.groups],
        [],
        1 << 30,
        6,
        fine_features,
        other,
        face_send,
        corner_send,
        coarse_grad,
    )
    received = [
        lax.ppermute(value, ("tx", "ty", "ch"), plan.pairs(first, second))
        for value, (first, second) in zip(sent, plan.groups)
    ]
    split = [g for g, (first, second) in enumerate(plan.groups) if first != second]
    work = 2 * wide * half * LOW
    befores = []
    early_table, first = table, 0
    for step, count in enumerate(plan.early):
        (before,) = call(
            functools.partial(own_gather_kernel, plan, first, count),
            "own_gather",
            [((wide, count * LOW), BF)],
            [],
            work * plan.own_blocks * count * LOW // half,
            16,
            early_table,
            high,
            low,
        )
        befores.append(before)
        first += count
        if step == 0:
            early_table, before, *ready = lax.optimization_barrier(
                (table, before, *[received[g] for g in split])
            )
            befores[0] = before
            for g, value in zip(split, ready):
                received[g] = value
            swapped = [swap(received[g]) for g in split]
    weight = conv_weight.reshape(wide, n)
    owners = plan.slots + 1
    across = plan.sum_width + owners * m
    grad, mine, theirs = run(
        middle_kernel,
        "middle",
        [((n, half), BF), ((s, across), F32), ((s, across), F32)],
        [
            (((plan.own_blocks + plan.halo_blocks) * n, LOW), BF),
            ((wide, half), BF),
            ((plan.coarse_channels, owners * m), BF),
            ((owners * n, m), BF),
            ((n, plan.padded), F32),
            ((owners * n, m), F32),
            ((n, plan.sum_width - plan.padded), F32),
        ],
        work * (plan.own_blocks + plan.halo_blocks),
        24,
        *received,
        *swapped,
        *befores,
        table,
        high,
        low,
        owner_side.reshape(1, -1),
        owner_slot.reshape(1, -1),
        weight,
        coarse_weight,
        coarse_grad,
    )
    theirs = swap(theirs)
    (halo,) = run(
        halo_scatter_kernel,
        "halo_scatter",
        [((plan.halo_blocks * n, LOW), F32)],
        [((wide, half), BF)],
        work * plan.halo_blocks,
        16,
        weight,
        grad,
        high,
        low,
    )
    message = plan.sum_width // (n // s) + m // (n // s) + max(plan.widths)
    joined, send = run(
        join_kernel,
        "join",
        [((s, across), F32), ((plan.tiles, n, message), BF)],
        [],
        1 << 20,
        6,
        mine,
        theirs,
        halo,
    )
    arrived = lax.all_to_all(send, ("tx", "ty"), 0, 0, tiled=True)
    (total,) = run(
        own_scatter_kernel,
        "own_scatter",
        [((plan.own_blocks * n, LOW), F32)],
        [((wide, half), BF)],
        work * plan.own_blocks,
        16,
        weight,
        grad,
        high,
        low,
    )
    share = plan.coarse_share
    mine, theirs, coarse_mine, coarse_theirs, conv_weight_grad, coarse_weight_grad = run(
        final_kernel,
        "final",
        [((s, plan.voxels), F32)] * 2 + [((share, m), F32)] * 2 + [((plan.offsets, s, n), F32), ((n, share), F32)],
        [((plan.own_blocks * n, LOW), F32), ((plan.coarse_channels, m), F32)],
        1 << 30,
        12,
        total,
        joined,
        arrived,
        face_send,
        corner_send,
        coarse_weight,
    )
    input_grad, coarse_out = run(
        add_kernel,
        "add",
        [((s, plan.voxels), BF), ((share, m), BF)],
        [],
        1 << 20,
        6,
        mine,
        swap(theirs),
        coarse_mine,
        swap(coarse_theirs),
    )
    return (coarse_out, input_grad, conv_weight_grad.transpose(0, 2, 1), coarse_weight_grad)


def solution(mesh):
    tiles = ("group", "tx", "ty")
    in_specs = (
        P("ch", tiles),
        P(None, tiles),
        P(None, tiles),
        P(None, tiles),
        P(tiles),
        P(tiles),
        P(),
        P(),
        P(None, tiles),
    )
    out_specs = (
        P("ch", tiles),
        P("ch", tiles),
        P("group", None, "ch"),
        P("group", "ch"),
    )
    return jax.shard_map(shards, mesh=mesh, in_specs=in_specs, out_specs=out_specs, check_vma=False)
```

```python
import functools

import jax
import jax.numpy as jnp
from jax import lax
from jax.experimental import pallas as pl
from jax.experimental.pallas import tpu as pltpu
from jax.sharding import PartitionSpec as P

BF = jnp.bfloat16
F32 = jnp.float32
STEPS = ((-1, 0), (1, 0), (0, -1), (0, 1), (-1, -1), (-1, 1), (1, -1), (1, 1))
LOW = 256


def call(kernel, name, outs, scratch, flops, mib, *args):
    return pl.pallas_call(
        kernel,
        name=name,
        out_shape=[jax.ShapeDtypeStruct(s, d) for s, d in outs],
        in_specs=[pl.BlockSpec(memory_space=pltpu.VMEM)] * len(args),
        out_specs=[pl.BlockSpec(memory_space=pltpu.VMEM)] * len(outs),
        scratch_shapes=[pltpu.VMEM(s, d) for s, d in scratch],
        compiler_params=pltpu.CompilerParams(vmem_limit_bytes=mib << 20),
        cost_estimate=pl.CostEstimate(flops=flops, bytes_accessed=1 << 20, transcendentals=0),
    )(*args)


class Plan:
    def __init__(self, shapes, nx, ny, nch):
        features, neighbours, face_send, corner_send, coarse_weight, coarse_grad = shapes
        self.nx, self.ny, self.nch = nx, ny, nch
        self.share, self.voxels = features
        self.channels = self.share * nch
        self.offsets = neighbours[0]
        self.half = self.voxels // nch
        self.face, self.corner = face_send[1], corner_send[1]
        self.coarse_channels, self.coarse = coarse_grad
        self.coarse_share = self.coarse_channels // nch
        self.own_blocks = self.voxels // LOW
        self.paired = ny == 2
        self.widths = [self.face] * (3 if self.paired else 4)
        self.widths += [self.corner] * (2 if self.paired else 4)
        self.slots = len(self.widths)
        self.halo = sum(self.widths)
        self.halo_blocks = self.halo // LOW
        self.starts = [sum(self.widths[:s]) for s in range(self.slots)]
        self.nothing = self.voxels + self.halo
        self.wrapped = self.paired and nx % 2 == 0
        self.itself = self.offsets // 2
        self.tiles = nx * ny
        self.groups = ((0, 1), (3, 4), (2, 2)) if self.paired else ((0, 1), (2, 3), (4, 5), (6, 7))
        self.swaps = sum(a != b for a, b in self.groups)
        self.early = (2, 1)
        self.padded = -(-self.offsets * self.channels // 128) * 128
        self.sum_width = self.padded + self.coarse_channels * self.channels // nch // self.share

    def directions(self, slot):
        if self.paired:
            return ((0,), (1,), (2, 3), (4, 5), (6, 7))[slot]
        return (slot,)

    def is_first(self, core, x):
        return (core + x) % 2 == 1 if self.paired else core == 0

    def pairs(self, first, second):
        found = []
        for core in range(self.nch):
            for x in range(self.nx):
                for y in range(self.ny):
                    for d in self.directions(first if self.is_first(core, x) else second):
                        sx, sy = x + STEPS[d][0], y + STEPS[d][1]
                        if self.wrapped:
                            sx %= self.nx
                        if 0 <= sx < self.nx and 0 <= sy < self.ny:
                            here, there = x * self.ny + y, sx * self.ny + sy
                            found.append((there * self.nch + core, here * self.nch + core))
        return found

    def sent_first(self, core, x):
        return jnp.logical_not(self.is_first(core, x)) if self.paired else self.is_first(core, x)

    def opposite(self, slot):
        return ((1, 0, 2, 4, 3) if self.paired else (1, 0, 3, 2, 7, 6, 5, 4))[slot]

    def bordering(self, slot, x, y):
        step = STEPS[self.directions(slot)[0]]
        to_x = x + step[0]
        there = (to_x >= 0) & (to_x < self.nx)
        if self.paired:
            to_y = 1 - y if step[1] else y
        else:
            to_y = y + step[1]
            there = there & (to_y >= 0) & (to_y < self.ny)
        return jnp.where(there, to_x * self.ny + to_y, -1)

    def send_rows(self, slot, y, face, corner):
        if not self.paired:
            if slot < 4:
                index = (1, 0, 3, 2)[slot]
                return face[index : index + 1, :]
            index = (3, 2, 1, 0)[slot - 4]
            return corner[index : index + 1, :]
        if slot == 0:
            return face[1:2, :]
        if slot == 1:
            return face[0:1, :]
        if slot == 2:
            return jnp.where(y == 0, face[3:4, :], face[2:3, :])
        if slot == 3:
            return jnp.where(y == 0, corner[3:4, :], corner[2:3, :])
        return jnp.where(y == 0, corner[1:2, :], corner[0:1, :])

    def rows(self, index, y):
        if not self.paired:
            return jnp.minimum(index, self.nothing)
        v, f, c = self.voxels, self.face, self.corner
        along_y = v + 2 * f
        corners = v + 4 * f
        end = corners + 4 * c
        mine = jnp.where(y == 0, along_y + f, along_y)
        of_y = jnp.where((index >= mine) & (index < mine + f), index - mine + along_y, self.nothing)
        result = jnp.where(index < along_y, index, of_y)
        first = jnp.where(y == 0, c, 0)
        at = index - corners - first
        one = jnp.where((at >= 0) & (at < c), at + v + 3 * f, self.nothing)
        two = jnp.where((at >= 2 * c) & (at < 3 * c), at - c + v + 3 * f, one)
        return jnp.where((index >= corners) & (index < end), two, result)

    def owner_slots(self, side):
        if not self.paired:
            return side
        return jnp.where(side < 3, side, jnp.where(side < 5, 3, jnp.where(side < 7, 4, 5)))


def lows(low, height, width):
    iota = lax.broadcasted_iota(jnp.int32, (height, width), 0).astype(BF)
    return jnp.where(iota == low, BF(1), BF(0))


def where_am_i(plan):
    core, x, y = (lax.axis_index(a) for a in ("ch", "tx", "ty"))
    return core, x, y


def prepare_kernel(plan, neighbours, high_out, low_out):
    core, _, y = where_am_i(plan)
    mine = pl.ds(pl.multiple_of(core * plan.half, plan.half), plan.half)
    rows = plan.rows(neighbours[:, mine], y)
    pad = high_out.shape[0] - plan.offsets
    fill = jnp.zeros((pad, plan.half), jnp.int32)
    rows = jnp.concatenate([rows, fill], axis=0) if pad else rows
    high_out[...] = lax.shift_right_logical(rows, 8).astype(F32)
    low_out[...] = (rows & (LOW - 1)).astype(F32)


def pack_kernel(plan, own, other, face, corner, coarse_grad, table, *messages):
    core, x, y = where_am_i(plan)
    s, n = plan.share, plan.channels
    at_own = pl.multiple_of(core * s, s)
    at_other = pl.multiple_of((1 - core) * s, s)
    for b in range(plan.own_blocks):
        table[pl.ds(b * n + at_own, s), :] = own[:, b * LOW : (b + 1) * LOW]
        table[pl.ds(b * n + at_other, s), :] = other[:, b * LOW : (b + 1) * LOW]
    groups = plan.coarse_channels // n
    for g, (first, second) in enumerate(plan.groups):
        width = plan.widths[first]
        rows = plan.send_rows(first, y, face, corner)
        if second != first:
            rows = jnp.where(plan.sent_first(core, x), rows, plan.send_rows(second, y, face, corner))
        high = lax.shift_right_logical(rows, 8)
        hot = lows((rows & (LOW - 1)).astype(F32).astype(BF), LOW, width)
        part = jnp.dot(table[...], hot, preferred_element_type=F32)
        picked = jnp.zeros((n, width), F32)
        for b in range(plan.own_blocks):
            picked = jnp.where(high == b, part[b * n : (b + 1) * n], picked)
        messages[g][:, :width] = picked.astype(BF)
        for q in range(groups):
            at = width + q * plan.coarse
            messages[g][:, at : at + plan.coarse] = coarse_grad[q * n : (q + 1) * n, :]


def gather_block(plan, table, high_ref, low_ref, out, fs, base, blocks, to=None, before=None):
    to = fs if to is None else to
    n = plan.channels
    for k in range(plan.offsets):
        if k == plan.itself:
            continue
        at = slice(k * n, (k + 1) * n)
        low = low_ref[k : k + 1, fs].astype(BF)
        high = high_ref[k : k + 1, fs]
        part = jnp.dot(table[...], lows(low, LOW, LOW), preferred_element_type=F32)
        if before is None:
            picked = jnp.zeros((n, LOW), F32)
        else:
            picked = before[at, to].astype(F32)
        for b in range(blocks):
            picked = jnp.where(high == float(base + b), part[b * n : (b + 1) * n], picked)
        out[at, fs if before is not None else to] = picked.astype(BF)


def columns(block):
    if isinstance(block, int):
        return slice(block * LOW, (block + 1) * LOW)
    return pl.ds(pl.multiple_of(block * LOW, LOW), LOW)


def blocks_loop(first, last, body):
    pairs = (last - first) // 2

    def two(j, carry):
        body(first + 2 * j)
        body(first + 2 * j + 1)
        return carry

    if pairs > 1:
        lax.fori_loop(0, pairs, two, 0)
    elif pairs:
        two(0, 0)
    if (last - first) % 2:
        body(last - 1)


def own_gather_kernel(plan, first, count, table, high, low, out):
    def body(j):
        to = columns(j - first)
        gather_block(plan, table, high, low, out, columns(j), 0, plan.own_blocks, to)

    blocks_loop(first, first + count, body)


def middle_kernel(plan, *refs):
    n, s, m = plan.channels, plan.share, plan.coarse
    count = len(plan.groups)
    received, refs = refs[:count], refs[count:]
    swapped, refs = refs[: plan.swaps], refs[plan.swaps :]
    befores, refs = refs[: len(plan.early)], refs[len(plan.early) :]
    own_table, high, low, side, slot, weight, coarse_weight, coarse_grad, refs = (*refs[:8], refs[8:])
    grad_out, mine_out, theirs_out, table, rows, coarse_all, pooled_all, sums, parts, coarse_sum = refs
    core, x, y = where_am_i(plan)
    is_first = plan.is_first(core, x)
    messages = {}
    other = iter(swapped)
    for g, (first, second) in enumerate(plan.groups):
        here = received[g][...]
        if first == second:
            messages[first] = here
        else:
            there = next(other)[...]
            messages[first] = jnp.where(is_first, here, there)
            messages[second] = jnp.where(is_first, there, here)
    if plan.wrapped:
        for k in range(plan.slots):
            here = messages[k]
            messages[k] = jnp.where(plan.bordering(k, x, y) >= 0, here, jnp.zeros_like(here))
    own = plan.own_blocks * n
    table[:own, :] = own_table[...]
    for k in range(plan.slots):
        for part in range(0, plan.widths[k], min(LOW, plan.widths[k])):
            width = min(LOW, plan.widths[k])
            at = plan.starts[k] + part
            b, column = at // LOW, at % LOW
            table[own + b * n : own + (b + 1) * n, column : column + width] = messages[k][
                :, part : part + width
            ]
    groups = plan.coarse_channels // n
    coarse_all[:, :m] = coarse_grad[...]
    for k in range(plan.slots):
        for g in range(groups):
            at = plan.widths[k] + g * m
            coarse_all[g * n : (g + 1) * n, (k + 1) * m : (k + 2) * m] = messages[k][:, at : at + m]

    halo_table = table.at[own:, :]
    done = 0
    for before, count in zip(befores, plan.early):

        def rest(j):
            of = columns(j - done)
            gather_block(
                plan, halo_table, high, low, rows, columns(j), plan.own_blocks, plan.halo_blocks, of, before
            )

        blocks_loop(done, done + count, rest)
        done += count

    def whole(j):
        gather_block(plan, table, high, low, rows, columns(j), 0, plan.own_blocks + plan.halo_blocks)

    blocks_loop(done, plan.half // LOW, whole)
    for j in range(plan.half // LOW):
        at = pl.multiple_of((core * (plan.half // LOW) + j) * n, n)
        rows[plan.itself * n : (plan.itself + 1) * n, j * LOW : (j + 1) * LOW] = table[pl.ds(at, n), :]

    grads = jnp.dot(coarse_weight[...], coarse_all[...], preferred_element_type=F32).astype(BF)
    owners = plan.slots + 1
    for k in range(owners):
        pooled_all[k * n : (k + 1) * n, :] = grads[:, k * m : (k + 1) * m]
    chunk = min(plan.half, 1024)
    wide = plan.offsets * n
    sums[...] = jnp.zeros_like(sums)
    parts[...] = jnp.zeros_like(parts)
    for c in range(plan.half // chunk):
        fs = slice(c * chunk, (c + 1) * chunk)
        picked = rows[:, fs]
        hidden = lax.dot_general(
            weight[...], picked, (((0,), (0,)), ((), ())), preferred_element_type=F32
        )
        sigma = 1.0 / (1.0 + jnp.exp(-hidden))
        active = (hidden * sigma).astype(BF)
        mine = pl.ds(pl.multiple_of(core * plan.half + c * chunk, LOW), chunk)
        owner = plan.owner_slots(side[:, mine]).astype(F32)
        owner_low = owner.astype(BF)
        hot = lows(slot[:, mine].astype(F32).astype(BF), m, chunk)
        spread = jnp.concatenate(
            [jnp.where(owner_low == BF(k), active, BF(0)) for k in range(owners)], axis=0
        )
        parts[...] += lax.dot_general(
            spread, hot, (((1,), (1,)), ((), ())), preferred_element_type=F32
        )
        found = jnp.dot(pooled_all[...], hot, preferred_element_type=F32)
        above = jnp.zeros((n, chunk), F32)
        for k in range(owners):
            above = jnp.where(owner == float(k), found[k * n : (k + 1) * n], above)
        grad = (above * (sigma * (1.0 + hidden * (1.0 - sigma)))).astype(BF)
        grad_out[:, fs] = grad
        sums[:, :wide] += lax.dot_general(
            grad, picked, (((1,), (1,)), ((), ())), preferred_element_type=F32
        )
    total = jnp.zeros((n, plan.coarse_channels), F32)
    for k in range(owners):
        value = parts[k * n : (k + 1) * n, :]
        first = value.astype(BF)
        second = (value - first.astype(F32)).astype(BF)
        grads_k = coarse_all[:, k * m : (k + 1) * m]
        for piece in (first, second):
            total = total + lax.dot_general(
                piece, grads_k, (((1,), (1,)), ((), ())), preferred_element_type=F32
            )
    for h in range(plan.nch):
        half = total[:, h * plan.coarse_share : (h + 1) * plan.coarse_share]
        for q in range(n // s):
            at = q * plan.coarse_share
            coarse_sum[h * s : (h + 1) * s, at : at + plan.coarse_share] = half[q * s : (q + 1) * s]
    at_own = pl.multiple_of(core * s, s)
    at_other = pl.multiple_of((1 - core) * s, s)
    padded = sums.shape[1]
    after = padded + coarse_sum.shape[1]
    for out, at in ((mine_out, at_own), (theirs_out, at_other)):
        out[:, :padded] = sums[pl.ds(at, s), :]
        out[:, padded:after] = coarse_sum[pl.ds(at, s), :]
        for k in range(owners):
            out[:, after + k * m : after + (k + 1) * m] = parts[pl.ds(k * n + at, s), :]


def scatter_loop(plan, values, high_ref, low_ref, total, base, blocks):
    n = plan.channels
    total[...] = jnp.zeros_like(total)

    width = min(plan.half, 2 * LOW)

    def body(j, carry):
        fs = pl.ds(pl.multiple_of(j * width, width), width)
        masked, hots = [], []
        for k in range(plan.offsets):
            if k == plan.itself:
                continue
            high = high_ref[k : k + 1, fs].astype(BF)
            hots.append(lows(low_ref[k : k + 1, fs].astype(BF), LOW, width))
            value = values[k * n : (k + 1) * n, fs]
            masked.append(
                jnp.concatenate(
                    [jnp.where(high == BF(base + b), value, BF(0)) for b in range(blocks)], axis=0
                )
            )
        total[...] += lax.dot_general(
            jnp.concatenate(masked, axis=1),
            jnp.concatenate(hots, axis=1),
            (((1,), (1,)), ((), ())),
            preferred_element_type=F32,
        )
        return carry

    lax.fori_loop(0, plan.half // width, body, 0)


def spread_values(plan, weight, grad, values):
    chunk = min(plan.half, 512)
    for c in range(plan.half // chunk):
        fs = slice(c * chunk, (c + 1) * chunk)
        values[:, fs] = jnp.dot(weight[...], grad[:, fs], preferred_element_type=F32).astype(BF)


def halo_scatter_kernel(plan, weight, grad, high, low, total, values):
    spread_values(plan, weight, grad, values)
    scatter_loop(plan, values, high, low, total, plan.own_blocks, plan.halo_blocks)


def join_kernel(plan, mine, theirs, halo, joined_out, send):
    _, x, y = where_am_i(plan)
    n, s, m = plan.channels, plan.share, plan.coarse
    joined_out[...] = mine[...] + theirs[...]
    width = plan.sum_width // (n // s)
    for t in range(plan.tiles):
        for q in range(n // s):
            send[t, q * s : (q + 1) * s, :width] = joined_out[:, q * width : (q + 1) * width].astype(BF)
    part = m // (n // s)
    for k in range(plan.slots):
        tile = plan.bordering(k, x, y)

        @pl.when(tile >= 0)
        def _():
            at = plan.sum_width + (k + 1) * m
            for q in range(n // s):
                send[tile, q * s : (q + 1) * s, width : width + part] = joined_out[
                    :, at + q * part : at + (q + 1) * part
                ].astype(BF)
            size = min(LOW, plan.widths[k])
            for start in range(0, plan.widths[k], size):
                b, column = (plan.starts[k] + start) // LOW, (plan.starts[k] + start) % LOW
                to = width + part + start
                send[tile, :, to : to + size] = halo[b * n : (b + 1) * n, column : column + size].astype(BF)


def own_scatter_kernel(plan, weight, grad, high, low, total, values):
    core, _, _ = where_am_i(plan)
    n = plan.channels
    spread_values(plan, weight, grad, values)
    scatter_loop(plan, values, high, low, total, 0, plan.own_blocks)
    for j in range(plan.half // LOW):
        at = pl.ds(pl.multiple_of((core * (plan.half // LOW) + j) * n, n), n)
        total[at, :] += values[plan.itself * n : (plan.itself + 1) * n, j * LOW : (j + 1) * LOW].astype(F32)


def final_kernel(plan, total, joined, arrived, face, corner, coarse_weight, *refs):
    mine_out, theirs_out, coarse_mine, coarse_theirs, work, product = refs
    core, x, y = where_am_i(plan)
    n, s, m = plan.channels, plan.share, plan.coarse
    width = plan.sum_width // (n // s)
    part = m // (n // s)
    masked, hots = [], []
    pooled = joined[:, plan.sum_width : plan.sum_width + m]
    for k in range(plan.slots):
        tile = plan.bordering(k, x, y)
        there = tile >= 0
        tile = jnp.maximum(tile, 0)
        rows = plan.send_rows(plan.opposite(k), y, face, corner)
        high = lax.shift_right_logical(rows, 8).astype(F32).astype(BF)
        high = jnp.where(there, high, BF(-1))
        hots.append(lows((rows & (LOW - 1)).astype(F32).astype(BF), LOW, plan.widths[k]))
        value = arrived[tile, :, width + part : width + part + plan.widths[k]]
        masked.append(
            jnp.concatenate(
                [jnp.where(high == BF(b), value, BF(0)) for b in range(plan.own_blocks)], axis=0
            )
        )
        more = jnp.concatenate(
            [arrived[tile, q * s : (q + 1) * s, width : width + part] for q in range(n // s)], axis=1
        )
        pooled = pooled + jnp.where(there, more.astype(F32), 0.0)
    work[...] = total[...] + lax.dot_general(
        jnp.concatenate(masked, axis=1),
        jnp.concatenate(hots, axis=1),
        (((1,), (1,)), ((), ())),
        preferred_element_type=F32,
    )
    at_own = pl.multiple_of(core * s, s)
    at_other = pl.multiple_of((1 - core) * s, s)
    for b in range(plan.own_blocks):
        mine_out[:, b * LOW : (b + 1) * LOW] = work[pl.ds(b * n + at_own, s), :]
        theirs_out[:, b * LOW : (b + 1) * LOW] = work[pl.ds(b * n + at_other, s), :]
    share = plan.coarse_share
    product[...] = lax.dot_general(
        coarse_weight[pl.ds(at_own, s), :], pooled.astype(BF), (((0,), (0,)), ((), ())), preferred_element_type=F32
    )
    coarse_mine[...] = product[pl.ds(pl.multiple_of(core * share, share), share), :]
    coarse_theirs[...] = product[pl.ds(pl.multiple_of((1 - core) * share, share), share), :]


def sum_kernel(plan, arrived, mine, conv_out, coarse_grad_out):
    n, s, share = plan.channels, plan.share, plan.coarse_share
    width = plan.sum_width // (n // s)
    summed = arrived[0, :, :width].astype(F32)
    for t in range(1, plan.tiles):
        summed = summed + arrived[t, :, :width].astype(F32)
    summed = jnp.concatenate([summed[q * s : (q + 1) * s] for q in range(n // s)], axis=1)
    for k in range(plan.offsets):
        conv_out[k] = summed[:, k * n : (k + 1) * n]
    for q in range(n // s):
        at = plan.padded + q * share
        coarse_grad_out[q * s : (q + 1) * s, :] = summed[:, at : at + share]


def add_kernel(plan, mine, theirs, coarse_mine, coarse_theirs, out, coarse_out):
    out[...] = (mine[...] + theirs[...]).astype(BF)
    coarse_out[...] = (coarse_mine[...] + coarse_theirs[...]).astype(BF)


def shards(
    fine_features,
    neighbours,
    face_send,
    corner_send,
    owner_side,
    owner_slot,
    conv_weight,
    coarse_weight,
    coarse_grad,
):
    nx, ny, nch = (lax.axis_size(a) for a in ("tx", "ty", "ch"))
    plan = Plan(
        [
            a.shape
            for a in (fine_features, neighbours, face_send, corner_send, coarse_weight, coarse_grad)
        ],
        nx,
        ny,
        nch,
    )
    n, s, half, m = plan.channels, plan.share, plan.half, plan.coarse
    wide = plan.offsets * n

    def swap(value):
        return lax.ppermute(value, "ch", [(0, 1), (1, 0)])

    def run(kernel, name, outs, scratch, flops, mib, *args):
        return call(functools.partial(kernel, plan), name, outs, scratch, flops, mib, *args)

    other = swap(fine_features)
    tall = -(-plan.offsets // 8) * 8
    high, low = run(
        prepare_kernel,
        "prepare",
        [((tall, half), F32), ((tall, half), F32)],
        [],
        1 << 20,
        6,
        neighbours,
    )
    extra = plan.coarse_channels // n * m
    table, *sent = run(
        pack_kernel,
        "pack",
        [((plan.own_blocks * n, LOW), BF)]
        + [((n, plan.widths[first] + extra), BF) for first, _ in plan.groups],
        [],
        1 << 30,
        6,
        fine_features,
        other,
        face_send,
        corner_send,
        coarse_grad,
    )
    received = [
        lax.ppermute(value, ("tx", "ty", "ch"), plan.pairs(first, second))
        for value, (first, second) in zip(sent, plan.groups)
    ]
    split = [g for g, (first, second) in enumerate(plan.groups) if first != second]
    work = 2 * wide * half * LOW
    befores = []
    early_table, first = table, 0
    for step, count in enumerate(plan.early):
        (before,) = call(
            functools.partial(own_gather_kernel, plan, first, count),
            "own_gather",
            [((wide, count * LOW), BF)],
            [],
            work * plan.own_blocks * count * LOW // half,
            16,
            early_table,
            high,
            low,
        )
        befores.append(before)
        first += count
        if step == 0:
            early_table, before, *ready = lax.optimization_barrier(
                (table, before, *[received[g] for g in split])
            )
            befores[0] = before
            for g, value in zip(split, ready):
                received[g] = value
            swapped = [swap(received[g]) for g in split]
    weight = conv_weight.reshape(wide, n)
    owners = plan.slots + 1
    across = plan.sum_width + owners * m
    grad, mine, theirs = run(
        middle_kernel,
        "middle",
        [((n, half), BF), ((s, across), F32), ((s, across), F32)],
        [
            (((plan.own_blocks + plan.halo_blocks) * n, LOW), BF),
            ((wide, half), BF),
            ((plan.coarse_channels, owners * m), BF),
            ((owners * n, m), BF),
            ((n, plan.padded), F32),
            ((owners * n, m), F32),
            ((n, plan.sum_width - plan.padded), F32),
        ],
        work * (plan.own_blocks + plan.halo_blocks),
        24,
        *received,
        *swapped,
        *befores,
        table,
        high,
        low,
        owner_side.reshape(1, -1),
        owner_slot.reshape(1, -1),
        weight,
        coarse_weight,
        coarse_grad,
    )
    theirs = swap(theirs)
    (halo,) = run(
        halo_scatter_kernel,
        "halo_scatter",
        [((plan.halo_blocks * n, LOW), F32)],
        [((wide, half), BF)],
        work * plan.halo_blocks,
        16,
        weight,
        grad,
        high,
        low,
    )
    message = plan.sum_width // (n // s) + m // (n // s) + max(plan.widths)
    joined, send = run(
        join_kernel,
        "join",
        [((s, across), F32), ((plan.tiles, n, message), BF)],
        [],
        1 << 20,
        6,
        mine,
        theirs,
        halo,
    )
    arrived = lax.all_to_all(send, ("tx", "ty"), 0, 0, tiled=True)
    (total,) = run(
        own_scatter_kernel,
        "own_scatter",
        [((plan.own_blocks * n, LOW), F32)],
        [((wide, half), BF)],
        work * plan.own_blocks,
        16,
        weight,
        grad,
        high,
        low,
    )
    share = plan.coarse_share
    mine, theirs, coarse_mine, coarse_theirs = run(
        final_kernel,
        "final",
        [((s, plan.voxels), F32)] * 2 + [((share, m), F32)] * 2,
        [((plan.own_blocks * n, LOW), F32), ((plan.coarse_channels, m), F32)],
        1 << 30,
        12,
        total,
        joined,
        arrived,
        face_send,
        corner_send,
        coarse_weight,
    )
    conv_weight_grad, coarse_weight_grad = run(
        sum_kernel,
        "sum",
        [((plan.offsets, s, n), F32), ((n, share), F32)],
        [],
        1 << 28,
        6,
        arrived,
        coarse_mine,
    )
    input_grad, coarse_out = run(
        add_kernel,
        "add",
        [((s, plan.voxels), BF), ((share, m), BF)],
        [],
        1 << 20,
        6,
        mine,
        swap(theirs),
        coarse_mine,
        swap(coarse_theirs),
    )
    return (coarse_out, input_grad, conv_weight_grad.transpose(0, 2, 1), coarse_weight_grad)


def solution(mesh):
    tiles = ("group", "tx", "ty")
    in_specs = (
        P("ch", tiles),
        P(None, tiles),
        P(None, tiles),
        P(None, tiles),
        P(tiles),
        P(tiles),
        P(),
        P(),
        P(None, tiles),
    )
    out_specs = (
        P("ch", tiles),
        P("ch", tiles),
        P("group", None, "ch"),
        P("group", "ch"),
    )
    return jax.shard_map(shards, mesh=mesh, in_specs=in_specs, out_specs=out_specs, check_vma=False)
```

```python
import functools

import jax
import jax.numpy as jnp
from jax import lax
from jax.experimental import pallas as pl
from jax.experimental.pallas import tpu as pltpu
from jax.sharding import PartitionSpec as P

BF = jnp.bfloat16
F32 = jnp.float32
STEPS = ((-1, 0), (1, 0), (0, -1), (0, 1), (-1, -1), (-1, 1), (1, -1), (1, 1))
LOW = 256


def call(kernel, name, outs, scratch, flops, mib, *args):
    return pl.pallas_call(
        kernel,
        name=name,
        out_shape=[jax.ShapeDtypeStruct(s, d) for s, d in outs],
        in_specs=[pl.BlockSpec(memory_space=pltpu.VMEM)] * len(args),
        out_specs=[pl.BlockSpec(memory_space=pltpu.VMEM)] * len(outs),
        scratch_shapes=[pltpu.VMEM(s, d) for s, d in scratch],
        compiler_params=pltpu.CompilerParams(vmem_limit_bytes=mib << 20),
        cost_estimate=pl.CostEstimate(flops=flops, bytes_accessed=1 << 20, transcendentals=0),
    )(*args)


class Plan:
    def __init__(self, shapes, nx, ny, nch):
        features, neighbours, face_send, corner_send, coarse_weight, coarse_grad = shapes
        self.nx, self.ny, self.nch = nx, ny, nch
        self.share, self.voxels = features
        self.channels = self.share * nch
        self.offsets = neighbours[0]
        self.half = self.voxels // nch
        self.face, self.corner = face_send[1], corner_send[1]
        self.coarse_channels, self.coarse = coarse_grad
        self.coarse_share = self.coarse_channels // nch
        self.own_blocks = self.voxels // LOW
        self.paired = ny == 2
        self.widths = [self.face] * (3 if self.paired else 4)
        self.widths += [self.corner] * (2 if self.paired else 4)
        self.slots = len(self.widths)
        self.halo = sum(self.widths)
        self.halo_blocks = self.halo // LOW
        self.starts = [sum(self.widths[:s]) for s in range(self.slots)]
        self.nothing = self.voxels + self.halo
        self.wrapped = self.paired and nx % 2 == 0
        self.lane_blocks = 2
        self.itself = self.offsets // 2
        self.tiles = nx * ny
        self.groups = ((0, 1), (3, 4), (2, 2)) if self.paired else ((0, 1), (2, 3), (4, 5), (6, 7))
        self.swaps = sum(a != b for a, b in self.groups)
        self.early = (2, 1)
        self.padded = -(-self.offsets * self.channels // 128) * 128
        self.sum_width = self.padded + self.coarse_channels * self.channels // nch // self.share

    def directions(self, slot):
        if self.paired:
            return ((0,), (1,), (2, 3), (4, 5), (6, 7))[slot]
        return (slot,)

    def is_first(self, core, x):
        return (core + x) % 2 == 1 if self.paired else core == 0

    def pairs(self, first, second):
        found = []
        for core in range(self.nch):
            for x in range(self.nx):
                for y in range(self.ny):
                    for d in self.directions(first if self.is_first(core, x) else second):
                        sx, sy = x + STEPS[d][0], y + STEPS[d][1]
                        if self.wrapped:
                            sx %= self.nx
                        if 0 <= sx < self.nx and 0 <= sy < self.ny:
                            here, there = x * self.ny + y, sx * self.ny + sy
                            found.append((there * self.nch + core, here * self.nch + core))
        return found

    def sent_first(self, core, x):
        return jnp.logical_not(self.is_first(core, x)) if self.paired else self.is_first(core, x)

    def opposite(self, slot):
        return ((1, 0, 2, 4, 3) if self.paired else (1, 0, 3, 2, 7, 6, 5, 4))[slot]

    def bordering(self, slot, x, y):
        step = STEPS[self.directions(slot)[0]]
        to_x = x + step[0]
        there = (to_x >= 0) & (to_x < self.nx)
        if self.paired:
            to_y = 1 - y if step[1] else y
        else:
            to_y = y + step[1]
            there = there & (to_y >= 0) & (to_y < self.ny)
        return jnp.where(there, to_x * self.ny + to_y, -1)

    def send_rows(self, slot, y, face, corner):
        if not self.paired:
            if slot < 4:
                index = (1, 0, 3, 2)[slot]
                return face[index : index + 1, :]
            index = (3, 2, 1, 0)[slot - 4]
            return corner[index : index + 1, :]
        if slot == 0:
            return face[1:2, :]
        if slot == 1:
            return face[0:1, :]
        if slot == 2:
            return jnp.where(y == 0, face[3:4, :], face[2:3, :])
        if slot == 3:
            return jnp.where(y == 0, corner[3:4, :], corner[2:3, :])
        return jnp.where(y == 0, corner[1:2, :], corner[0:1, :])

    def rows(self, index, y):
        if not self.paired:
            return jnp.minimum(index, self.nothing)
        v, f, c = self.voxels, self.face, self.corner
        along_y = v + 2 * f
        corners = v + 4 * f
        end = corners + 4 * c
        mine = jnp.where(y == 0, along_y + f, along_y)
        of_y = jnp.where((index >= mine) & (index < mine + f), index - mine + along_y, self.nothing)
        result = jnp.where(index < along_y, index, of_y)
        first = jnp.where(y == 0, c, 0)
        at = index - corners - first
        one = jnp.where((at >= 0) & (at < c), at + v + 3 * f, self.nothing)
        two = jnp.where((at >= 2 * c) & (at < 3 * c), at - c + v + 3 * f, one)
        return jnp.where((index >= corners) & (index < end), two, result)

    def owner_slots(self, side):
        if not self.paired:
            return side
        return jnp.where(side < 3, side, jnp.where(side < 5, 3, jnp.where(side < 7, 4, 5)))


def lows(low, height, width):
    iota = lax.broadcasted_iota(jnp.int32, (height, width), 0).astype(BF)
    return jnp.where(iota == low, BF(1), BF(0))


def where_am_i(plan):
    core, x, y = (lax.axis_index(a) for a in ("ch", "tx", "ty"))
    return core, x, y


def prepare_kernel(plan, neighbours, high_out, low_out):
    core, _, y = where_am_i(plan)
    mine = pl.ds(pl.multiple_of(core * plan.half, plan.half), plan.half)
    rows = plan.rows(neighbours[:, mine], y)
    pad = high_out.shape[0] - plan.offsets
    fill = jnp.zeros((pad, plan.half), jnp.int32)
    rows = jnp.concatenate([rows, fill], axis=0) if pad else rows
    high_out[...] = lax.shift_right_logical(rows, 8).astype(F32)
    low_out[...] = (rows & (LOW - 1)).astype(F32)


def pack_kernel(plan, own, other, face, corner, coarse_grad, table, *messages):
    core, x, y = where_am_i(plan)
    s, n = plan.share, plan.channels
    at_own = pl.multiple_of(core * s, s)
    at_other = pl.multiple_of((1 - core) * s, s)
    for b in range(plan.own_blocks):
        table[pl.ds(b * n + at_own, s), :] = own[:, b * LOW : (b + 1) * LOW]
        table[pl.ds(b * n + at_other, s), :] = other[:, b * LOW : (b + 1) * LOW]
    groups = plan.coarse_channels // n
    for g, (first, second) in enumerate(plan.groups):
        width = plan.widths[first]
        rows = plan.send_rows(first, y, face, corner)
        if second != first:
            rows = jnp.where(plan.sent_first(core, x), rows, plan.send_rows(second, y, face, corner))
        high = lax.shift_right_logical(rows, 8)
        hot = lows((rows & (LOW - 1)).astype(F32).astype(BF), LOW, width)
        part = jnp.dot(table[...], hot, preferred_element_type=F32)
        picked = jnp.zeros((n, width), F32)
        for b in range(plan.own_blocks):
            picked = jnp.where(high == b, part[b * n : (b + 1) * n], picked)
        messages[g][:, :width] = picked.astype(BF)
        for q in range(groups):
            at = width + q * plan.coarse
            messages[g][:, at : at + plan.coarse] = coarse_grad[q * n : (q + 1) * n, :]


def gather_block(plan, table, high_ref, low_ref, out, fs, base, blocks, to=None, before=None, side=None):
    to = fs if to is None else to
    n = plan.channels
    for k in range(plan.offsets):
        if k == plan.itself:
            continue
        at = slice(k * n, (k + 1) * n)
        low = low_ref[k : k + 1, fs].astype(BF)
        high = high_ref[k : k + 1, fs]
        part = jnp.dot(table[...], lows(low, LOW, LOW), preferred_element_type=F32)
        if before is None:
            picked = jnp.zeros((n, LOW), F32)
        else:
            picked = before[at, to].astype(F32)
        if side is not None:
            picked = pick_lanes(side, high, low_ref[k : k + 1, fs], base + blocks, n)
        for b in range(blocks):
            picked = jnp.where(high == float(base + b), part[b * n : (b + 1) * n], picked)
        out[at, fs if before is not None else to] = picked.astype(BF)


def pick_lanes(side, high, low, base, n):
    upper = low >= 128.0
    row = jnp.broadcast_to(2.0 * (high - float(base)) + jnp.where(upper, 1.0, 0.0), (8, LOW))
    lane = jnp.broadcast_to((low - jnp.where(upper, 128.0, 0.0)).astype(jnp.int32), (8, LOW))
    across = []
    for q in range(LOW // 128):
        at = slice(q * 128, (q + 1) * 128)
        down = []
        for c in range(0, n, 8):
            found = jnp.zeros((8, 128), F32)
            for b in range(side.shape[1] // 128):
                source = side[c : c + 8, b * 128 : (b + 1) * 128]
                found = jnp.where(row[:, at] == float(b), jnp.take_along_axis(source, lane[:, at], axis=1), found)
            down.append(found)
        across.append(jnp.concatenate(down, axis=0))
    return jnp.concatenate(across, axis=1)


def columns(block):
    if isinstance(block, int):
        return slice(block * LOW, (block + 1) * LOW)
    return pl.ds(pl.multiple_of(block * LOW, LOW), LOW)


def blocks_loop(first, last, body):
    pairs = (last - first) // 2

    def two(j, carry):
        body(first + 2 * j)
        body(first + 2 * j + 1)
        return carry

    if pairs > 1:
        lax.fori_loop(0, pairs, two, 0)
    elif pairs:
        two(0, 0)
    if (last - first) % 2:
        body(last - 1)


def own_gather_kernel(plan, first, count, table, high, low, out):
    def body(j):
        to = columns(j - first)
        gather_block(plan, table, high, low, out, columns(j), 0, plan.own_blocks, to)

    blocks_loop(first, first + count, body)


def middle_kernel(plan, *refs):
    n, s, m = plan.channels, plan.share, plan.coarse
    count = len(plan.groups)
    received, refs = refs[:count], refs[count:]
    swapped, refs = refs[: plan.swaps], refs[plan.swaps :]
    befores, refs = refs[: len(plan.early)], refs[len(plan.early) :]
    own_table, high, low, side, slot, weight, coarse_weight, coarse_grad, refs = (*refs[:8], refs[8:])
    grad_out, mine_out, theirs_out, table, rows, coarse_all, pooled_all, sums, parts, coarse_sum, lanes = refs
    core, x, y = where_am_i(plan)
    is_first = plan.is_first(core, x)
    messages = {}
    other = iter(swapped)
    for g, (first, second) in enumerate(plan.groups):
        here = received[g][...]
        if first == second:
            messages[first] = here
        else:
            there = next(other)[...]
            messages[first] = jnp.where(is_first, here, there)
            messages[second] = jnp.where(is_first, there, here)
    if plan.wrapped:
        for k in range(plan.slots):
            here = messages[k]
            messages[k] = jnp.where(plan.bordering(k, x, y) >= 0, here, jnp.zeros_like(here))
    own = plan.own_blocks * n
    table[:own, :] = own_table[...]
    for k in range(plan.slots):
        for part in range(0, plan.widths[k], min(LOW, plan.widths[k])):
            width = min(LOW, plan.widths[k])
            at = plan.starts[k] + part
            b, column = at // LOW, at % LOW
            table[own + b * n : own + (b + 1) * n, column : column + width] = messages[k][
                :, part : part + width
            ]
    groups = plan.coarse_channels // n
    coarse_all[:, :m] = coarse_grad[...]
    for k in range(plan.slots):
        for g in range(groups):
            at = plan.widths[k] + g * m
            coarse_all[g * n : (g + 1) * n, (k + 1) * m : (k + 2) * m] = messages[k][:, at : at + m]

    halo_table = table.at[own:, :]
    done = 0
    for before, count in zip(befores, plan.early):

        def rest(j):
            of = columns(j - done)
            gather_block(
                plan, halo_table, high, low, rows, columns(j), plan.own_blocks, plan.halo_blocks, of, before
            )

        blocks_loop(done, done + count, rest)
        done += count

    main = plan.own_blocks + plan.halo_blocks - plan.lane_blocks
    main_table = table.at[: main * n, :]
    for b in range(plan.lane_blocks):
        lanes[:, b * LOW : (b + 1) * LOW] = table[(main + b) * n : (main + b + 1) * n, :].astype(F32)

    def whole(j):
        gather_block(plan, main_table, high, low, rows, columns(j), 0, main, side=lanes)

    blocks_loop(done, plan.half // LOW, whole)
    for j in range(plan.half // LOW):
        at = pl.multiple_of((core * (plan.half // LOW) + j) * n, n)
        rows[plan.itself * n : (plan.itself + 1) * n, j * LOW : (j + 1) * LOW] = table[pl.ds(at, n), :]

    grads = jnp.dot(coarse_weight[...], coarse_all[...], preferred_element_type=F32).astype(BF)
    owners = plan.slots + 1
    for k in range(owners):
        pooled_all[k * n : (k + 1) * n, :] = grads[:, k * m : (k + 1) * m]
    chunk = min(plan.half, 1024)
    wide = plan.offsets * n
    sums[...] = jnp.zeros_like(sums)
    parts[...] = jnp.zeros_like(parts)
    for c in range(plan.half // chunk):
        fs = slice(c * chunk, (c + 1) * chunk)
        picked = rows[:, fs]
        hidden = lax.dot_general(
            weight[...], picked, (((0,), (0,)), ((), ())), preferred_element_type=F32
        )
        sigma = 1.0 / (1.0 + jnp.exp(-hidden))
        active = (hidden * sigma).astype(BF)
        mine = pl.ds(pl.multiple_of(core * plan.half + c * chunk, LOW), chunk)
        owner = plan.owner_slots(side[:, mine]).astype(F32)
        owner_low = owner.astype(BF)
        hot = lows(slot[:, mine].astype(F32).astype(BF), m, chunk)
        spread = jnp.concatenate(
            [jnp.where(owner_low == BF(k), active, BF(0)) for k in range(owners)], axis=0
        )
        parts[...] += lax.dot_general(
            spread, hot, (((1,), (1,)), ((), ())), preferred_element_type=F32
        )
        found = jnp.dot(pooled_all[...], hot, preferred_element_type=F32)
        above = jnp.zeros((n, chunk), F32)
        for k in range(owners):
            above = jnp.where(owner == float(k), found[k * n : (k + 1) * n], above)
        grad = (above * (sigma * (1.0 + hidden * (1.0 - sigma)))).astype(BF)
        grad_out[:, fs] = grad
        sums[:, :wide] += lax.dot_general(
            grad, picked, (((1,), (1,)), ((), ())), preferred_element_type=F32
        )
    total = jnp.zeros((n, plan.coarse_channels), F32)
    for k in range(owners):
        value = parts[k * n : (k + 1) * n, :]
        first = value.astype(BF)
        second = (value - first.astype(F32)).astype(BF)
        grads_k = coarse_all[:, k * m : (k + 1) * m]
        for piece in (first, second):
            total = total + lax.dot_general(
                piece, grads_k, (((1,), (1,)), ((), ())), preferred_element_type=F32
            )
    for h in range(plan.nch):
        half = total[:, h * plan.coarse_share : (h + 1) * plan.coarse_share]
        for q in range(n // s):
            at = q * plan.coarse_share
            coarse_sum[h * s : (h + 1) * s, at : at + plan.coarse_share] = half[q * s : (q + 1) * s]
    at_own = pl.multiple_of(core * s, s)
    at_other = pl.multiple_of((1 - core) * s, s)
    padded = sums.shape[1]
    after = padded + coarse_sum.shape[1]
    for out, at in ((mine_out, at_own), (theirs_out, at_other)):
        out[:, :padded] = sums[pl.ds(at, s), :]
        out[:, padded:after] = coarse_sum[pl.ds(at, s), :]
        for k in range(owners):
            out[:, after + k * m : after + (k + 1) * m] = parts[pl.ds(k * n + at, s), :]


def scatter_loop(plan, values, high_ref, low_ref, total, base, blocks):
    n = plan.channels
    total[...] = jnp.zeros_like(total)

    width = min(plan.half, 2 * LOW)

    def body(j, carry):
        fs = pl.ds(pl.multiple_of(j * width, width), width)
        masked, hots = [], []
        for k in range(plan.offsets):
            if k == plan.itself:
                continue
            high = high_ref[k : k + 1, fs].astype(BF)
            hots.append(lows(low_ref[k : k + 1, fs].astype(BF), LOW, width))
            value = values[k * n : (k + 1) * n, fs]
            masked.append(
                jnp.concatenate(
                    [jnp.where(high == BF(base + b), value, BF(0)) for b in range(blocks)], axis=0
                )
            )
        total[...] += lax.dot_general(
            jnp.concatenate(masked, axis=1),
            jnp.concatenate(hots, axis=1),
            (((1,), (1,)), ((), ())),
            preferred_element_type=F32,
        )
        return carry

    lax.fori_loop(0, plan.half // width, body, 0)


def spread_values(plan, weight, grad, values):
    chunk = min(plan.half, 512)
    for c in range(plan.half // chunk):
        fs = slice(c * chunk, (c + 1) * chunk)
        values[:, fs] = jnp.dot(weight[...], grad[:, fs], preferred_element_type=F32).astype(BF)


def halo_scatter_kernel(plan, weight, grad, high, low, total, values):
    spread_values(plan, weight, grad, values)
    scatter_loop(plan, values, high, low, total, plan.own_blocks, plan.halo_blocks)


def join_kernel(plan, mine, theirs, halo, joined_out, send):
    _, x, y = where_am_i(plan)
    n, s, m = plan.channels, plan.share, plan.coarse
    joined_out[...] = mine[...] + theirs[...]
    width = plan.sum_width // (n // s)
    for t in range(plan.tiles):
        for q in range(n // s):
            send[t, q * s : (q + 1) * s, :width] = joined_out[:, q * width : (q + 1) * width].astype(BF)
    part = m // (n // s)
    for k in range(plan.slots):
        tile = plan.bordering(k, x, y)

        @pl.when(tile >= 0)
        def _():
            at = plan.sum_width + (k + 1) * m
            for q in range(n // s):
                send[tile, q * s : (q + 1) * s, width : width + part] = joined_out[
                    :, at + q * part : at + (q + 1) * part
                ].astype(BF)
            size = min(LOW, plan.widths[k])
            for start in range(0, plan.widths[k], size):
                b, column = (plan.starts[k] + start) // LOW, (plan.starts[k] + start) % LOW
                to = width + part + start
                send[tile, :, to : to + size] = halo[b * n : (b + 1) * n, column : column + size].astype(BF)


def own_scatter_kernel(plan, weight, grad, high, low, total, values):
    core, _, _ = where_am_i(plan)
    n = plan.channels
    spread_values(plan, weight, grad, values)
    scatter_loop(plan, values, high, low, total, 0, plan.own_blocks)
    for j in range(plan.half // LOW):
        at = pl.ds(pl.multiple_of((core * (plan.half // LOW) + j) * n, n), n)
        total[at, :] += values[plan.itself * n : (plan.itself + 1) * n, j * LOW : (j + 1) * LOW].astype(F32)


def final_kernel(plan, total, joined, arrived, face, corner, coarse_weight, *refs):
    mine_out, theirs_out, coarse_mine, coarse_theirs, work, product = refs
    core, x, y = where_am_i(plan)
    n, s, m = plan.channels, plan.share, plan.coarse
    width = plan.sum_width // (n // s)
    part = m // (n // s)
    masked, hots = [], []
    pooled = joined[:, plan.sum_width : plan.sum_width + m]
    for k in range(plan.slots):
        tile = plan.bordering(k, x, y)
        there = tile >= 0
        tile = jnp.maximum(tile, 0)
        rows = plan.send_rows(plan.opposite(k), y, face, corner)
        high = lax.shift_right_logical(rows, 8).astype(F32).astype(BF)
        high = jnp.where(there, high, BF(-1))
        hots.append(lows((rows & (LOW - 1)).astype(F32).astype(BF), LOW, plan.widths[k]))
        value = arrived[tile, :, width + part : width + part + plan.widths[k]]
        masked.append(
            jnp.concatenate(
                [jnp.where(high == BF(b), value, BF(0)) for b in range(plan.own_blocks)], axis=0
            )
        )
        more = jnp.concatenate(
            [arrived[tile, q * s : (q + 1) * s, width : width + part] for q in range(n // s)], axis=1
        )
        pooled = pooled + jnp.where(there, more.astype(F32), 0.0)
    work[...] = total[...] + lax.dot_general(
        jnp.concatenate(masked, axis=1),
        jnp.concatenate(hots, axis=1),
        (((1,), (1,)), ((), ())),
        preferred_element_type=F32,
    )
    at_own = pl.multiple_of(core * s, s)
    at_other = pl.multiple_of((1 - core) * s, s)
    for b in range(plan.own_blocks):
        mine_out[:, b * LOW : (b + 1) * LOW] = work[pl.ds(b * n + at_own, s), :]
        theirs_out[:, b * LOW : (b + 1) * LOW] = work[pl.ds(b * n + at_other, s), :]
    share = plan.coarse_share
    product[...] = lax.dot_general(
        coarse_weight[pl.ds(at_own, s), :], pooled.astype(BF), (((0,), (0,)), ((), ())), preferred_element_type=F32
    )
    coarse_mine[...] = product[pl.ds(pl.multiple_of(core * share, share), share), :]
    coarse_theirs[...] = product[pl.ds(pl.multiple_of((1 - core) * share, share), share), :]


def sum_kernel(plan, arrived, mine, conv_out, coarse_grad_out):
    n, s, share = plan.channels, plan.share, plan.coarse_share
    width = plan.sum_width // (n // s)
    summed = arrived[0, :, :width].astype(F32)
    for t in range(1, plan.tiles):
        summed = summed + arrived[t, :, :width].astype(F32)
    summed = jnp.concatenate([summed[q * s : (q + 1) * s] for q in range(n // s)], axis=1)
    for k in range(plan.offsets):
        conv_out[k] = summed[:, k * n : (k + 1) * n]
    for q in range(n // s):
        at = plan.padded + q * share
        coarse_grad_out[q * s : (q + 1) * s, :] = summed[:, at : at + share]


def add_kernel(plan, mine, theirs, coarse_mine, coarse_theirs, out, coarse_out):
    out[...] = (mine[...] + theirs[...]).astype(BF)
    coarse_out[...] = (coarse_mine[...] + coarse_theirs[...]).astype(BF)


def shards(
    fine_features,
    neighbours,
    face_send,
    corner_send,
    owner_side,
    owner_slot,
    conv_weight,
    coarse_weight,
    coarse_grad,
):
    nx, ny, nch = (lax.axis_size(a) for a in ("tx", "ty", "ch"))
    plan = Plan(
        [
            a.shape
            for a in (fine_features, neighbours, face_send, corner_send, coarse_weight, coarse_grad)
        ],
        nx,
        ny,
        nch,
    )
    n, s, half, m = plan.channels, plan.share, plan.half, plan.coarse
    wide = plan.offsets * n

    def swap(value):
        return lax.ppermute(value, "ch", [(0, 1), (1, 0)])

    def run(kernel, name, outs, scratch, flops, mib, *args):
        return call(functools.partial(kernel, plan), name, outs, scratch, flops, mib, *args)

    other = swap(fine_features)
    tall = -(-plan.offsets // 8) * 8
    high, low = run(
        prepare_kernel,
        "prepare",
        [((tall, half), F32), ((tall, half), F32)],
        [],
        1 << 20,
        6,
        neighbours,
    )
    extra = plan.coarse_channels // n * m
    table, *sent = run(
        pack_kernel,
        "pack",
        [((plan.own_blocks * n, LOW), BF)]
        + [((n, plan.widths[first] + extra), BF) for first, _ in plan.groups],
        [],
        1 << 30,
        6,
        fine_features,
        other,
        face_send,
        corner_send,
        coarse_grad,
    )
    received = [
        lax.ppermute(value, ("tx", "ty", "ch"), plan.pairs(first, second))
        for value, (first, second) in zip(sent, plan.groups)
    ]
    split = [g for g, (first, second) in enumerate(plan.groups) if first != second]
    work = 2 * wide * half * LOW
    befores = []
    early_table, first = table, 0
    for step, count in enumerate(plan.early):
        (before,) = call(
            functools.partial(own_gather_kernel, plan, first, count),
            "own_gather",
            [((wide, count * LOW), BF)],
            [],
            work * plan.own_blocks * count * LOW // half,
            16,
            early_table,
            high,
            low,
        )
        befores.append(before)
        first += count
        if step == 0:
            early_table, before, *ready = lax.optimization_barrier(
                (table, before, *[received[g] for g in split])
            )
            befores[0] = before
            for g, value in zip(split, ready):
                received[g] = value
            swapped = [swap(received[g]) for g in split]
    weight = conv_weight.reshape(wide, n)
    owners = plan.slots + 1
    across = plan.sum_width + owners * m
    grad, mine, theirs = run(
        middle_kernel,
        "middle",
        [((n, half), BF), ((s, across), F32), ((s, across), F32)],
        [
            (((plan.own_blocks + plan.halo_blocks) * n, LOW), BF),
            ((wide, half), BF),
            ((plan.coarse_channels, owners * m), BF),
            ((owners * n, m), BF),
            ((n, plan.padded), F32),
            ((owners * n, m), F32),
            ((n, plan.sum_width - plan.padded), F32),
            ((n, plan.lane_blocks * LOW), F32),
        ],
        work * (plan.own_blocks + plan.halo_blocks),
        24,
        *received,
        *swapped,
        *befores,
        table,
        high,
        low,
        owner_side.reshape(1, -1),
        owner_slot.reshape(1, -1),
        weight,
        coarse_weight,
        coarse_grad,
    )
    theirs = swap(theirs)
    (halo,) = run(
        halo_scatter_kernel,
        "halo_scatter",
        [((plan.halo_blocks * n, LOW), F32)],
        [((wide, half), BF)],
        work * plan.halo_blocks,
        16,
        weight,
        grad,
        high,
        low,
    )
    message = plan.sum_width // (n // s) + m // (n // s) + max(plan.widths)
    joined, send = run(
        join_kernel,
        "join",
        [((s, across), F32), ((plan.tiles, n, message), BF)],
        [],
        1 << 20,
        6,
        mine,
        theirs,
        halo,
    )
    arrived = lax.all_to_all(send, ("tx", "ty"), 0, 0, tiled=True)
    (total,) = run(
        own_scatter_kernel,
        "own_scatter",
        [((plan.own_blocks * n, LOW), F32)],
        [((wide, half), BF)],
        work * plan.own_blocks,
        16,
        weight,
        grad,
        high,
        low,
    )
    share = plan.coarse_share
    mine, theirs, coarse_mine, coarse_theirs = run(
        final_kernel,
        "final",
        [((s, plan.voxels), F32)] * 2 + [((share, m), F32)] * 2,
        [((plan.own_blocks * n, LOW), F32), ((plan.coarse_channels, m), F32)],
        1 << 30,
        12,
        total,
        joined,
        arrived,
        face_send,
        corner_send,
        coarse_weight,
    )
    conv_weight_grad, coarse_weight_grad = run(
        sum_kernel,
        "sum",
        [((plan.offsets, s, n), F32), ((n, share), F32)],
        [],
        1 << 28,
        6,
        arrived,
        coarse_mine,
    )
    input_grad, coarse_out = run(
        add_kernel,
        "add",
        [((s, plan.voxels), BF), ((share, m), BF)],
        [],
        1 << 20,
        6,
        mine,
        swap(theirs),
        coarse_mine,
        swap(coarse_theirs),
    )
    return (coarse_out, input_grad, conv_weight_grad.transpose(0, 2, 1), coarse_weight_grad)


def solution(mesh):
    tiles = ("group", "tx", "ty")
    in_specs = (
        P("ch", tiles),
        P(None, tiles),
        P(None, tiles),
        P(None, tiles),
        P(tiles),
        P(tiles),
        P(),
        P(),
        P(None, tiles),
    )
    out_specs = (
        P("ch", tiles),
        P("ch", tiles),
        P("group", None, "ch"),
        P("group", "ch"),
    )
    return jax.shard_map(shards, mesh=mesh, in_specs=in_specs, out_specs=out_specs, check_vma=False)
```
